128 devices in a mesh: src: 16 (over x, y), grp: 8 (over z, core).
Axes of the slice: x: 4, y: 4, z: 4, core: 2. Of those that a mesh axis runs over, the one named last changes fastest.
Arguments:
- embeds: bfloat16 [131072, 768], P(('src', 'grp')), may hold values from -6 to 6
- cluster_id: int32 [131072], P(('src', 'grp')), may hold values from 0 to 47, as said below
- cluster_rank: int32 [131072], P(('src', 'grp')), may hold values from 0 to 8189, as said below
- cluster_size: int32 [48], replicated, may hold values from 1 to 8190, as said below
Outputs:
- best: float32 [131072], P(('src', 'grp'))
The draws below stay inside these ranges and needn't reach their ends.
Inputs may be any that keep to these rules, and one draw needn't show every extreme that they name: `cluster_id`: every cluster id occurs; the clusters with ids g * 3 to g * 3 + 2 hold 8192 rows together. `cluster_rank`: within each cluster the ranks are 0 to its size minus one, each once. In the order by cluster and rank, no device's rows take more than 8 places of any aligned run of 512 places, and every aligned run of 1024 places has 16 places from some one device. cluster_size is the number of rows with each cluster id.
All inputs are finite; a program needn't handle non-finite values.
Results may differ from the reference program's by a relative error of at most 0.0013.
Values may be sent and summed in bfloat16 or wider, within the bound.
A program may use at most 128 MiB of HBM per device.

```python
import jax
import jax.numpy as jnp
from jax import lax

D = 768
R_DEV = 1024
CLU_GRP = 3
GROUP_ROWS = 8192
CLUSTERS = 48
ROWS = 131072
N_SRC = 16
DEVICES = 128


def layout(key):
    half_rows = R_DEV // 2
    mean_count = half_rows // DEVICES
    subkeys = jax.random.split(key, 5)
    lift = jax.random.randint(subkeys[0], (DEVICES // 2,), 0, mean_count + 1)
    lift = lift.at[0].set(mean_count).at[1].set(mean_count)
    counts = jnp.concatenate([mean_count + lift, mean_count - lift]).astype(jnp.int32)
    bounds = jnp.concatenate([jnp.zeros((1,), jnp.int32), jnp.cumsum(counts).astype(jnp.int32)])
    owners = jax.random.permutation(subkeys[1], DEVICES).astype(jnp.int32)
    shuffles = jax.vmap(lambda subkey: jax.random.permutation(subkey, half_rows))(jax.random.split(subkeys[2], 2 * DEVICES)).astype(jnp.int32)
    place_index = jnp.arange(ROWS, dtype=jnp.int32)
    piece_no = place_index // half_rows
    inner = shuffles[piece_no, place_index % half_rows]
    offset = jnp.sum((inner[:, None] >= bounds[None, 1:]).astype(jnp.int32), axis=1).astype(jnp.int32)
    klass = (piece_no + offset) % DEVICES
    source = owners[klass]
    turns = jnp.arange(DEVICES, dtype=jnp.int32)
    table = counts[(turns[:, None] - turns[None, :]) % DEVICES]
    before = (jnp.cumsum(table, axis=1) - table).astype(jnp.int32)
    order_no = piece_no // DEVICES * half_rows + before[klass, piece_no % DEVICES] + inner - bounds[offset]
    mixes = jax.vmap(lambda subkey: jax.random.permutation(subkey, R_DEV))(jax.random.split(subkeys[3], DEVICES)).astype(jnp.int32)
    final_slot = source * R_DEV + mixes[source, order_no]
    where_from = jnp.zeros((ROWS,), jnp.int32).at[final_slot].set(place_index)
    cuts = jax.vmap(lambda subkey: jnp.sort(jax.random.permutation(subkey, GROUP_ROWS - 1)[:CLU_GRP - 1] + 1))(jax.random.split(subkeys[4], N_SRC)).astype(jnp.int32)
    cuts = cuts.at[0].set(jnp.arange(1, CLU_GRP, dtype=jnp.int32))
    edges = jnp.concatenate([jnp.zeros((N_SRC, 1), jnp.int32), cuts, jnp.full((N_SRC, 1), GROUP_ROWS, jnp.int32)], axis=1)
    sizes = (edges[:, 1:] - edges[:, :-1]).reshape(CLUSTERS).astype(jnp.int32)
    group_of = place_index // GROUP_ROWS
    local_place = place_index % GROUP_ROWS
    member = jnp.sum((local_place[:, None] >= cuts[group_of]).astype(jnp.int32), axis=1).astype(jnp.int32)
    cluster = group_of * CLU_GRP + member
    ranks = local_place - edges[group_of, member]
    return (cluster[where_from].astype(jnp.int32), ranks[where_from].astype(jnp.int32), sizes)


def draw_cluster_id(key, part):
    return layout(key)[0]


def draw_cluster_rank(key, part):
    return layout(key)[1]


def draw_cluster_size(key, part):
    return layout(key)[2]


def level_of(key, shape, shards, low, top_value):
    def one(dim, parts):
        draws = jax.random.uniform(jax.random.fold_in(jax.random.fold_in(key, 6), dim), (parts,), jnp.float32, low / len(shards), top_value / len(shards))
        return jnp.repeat(jnp.exp(draws), shape[dim] // parts).reshape((-1,) + (1,) * (len(shape) - dim - 1))

    gain = one(*shards[0])
    for cut in shards[1:]:
        gain = gain * one(*cut)
    return gain


def normal_values(key, shape, deviation, most, cuts=(), kind=jnp.bfloat16):
    array = deviation * jax.random.normal(key, shape, jnp.float32)
    if cuts:
        array = array * level_of(key, shape, cuts, -0.22, 0.18)
    return jnp.clip(array, -most, most).astype(kind)


def setup_inputs(seed: int = 0) -> dict:
    streams_of = jax.random.split(jax.random.key(seed), 5)
    return {
        "embeds": normal_values(streams_of[0], (ROWS, D), 1.0, 6.0, ((0, 128),)),
        "cluster_id": draw_cluster_id(jax.random.fold_in(streams_of[4], 71), 0),
        "cluster_rank": draw_cluster_rank(jax.random.fold_in(streams_of[4], 71), 0),
        "cluster_size": draw_cluster_size(jax.random.fold_in(streams_of[4], 71), 0),
    }


epsilon = 1e-06

def reference(embeds, cluster_id, cluster_rank, cluster_size):
    widened = embeds.astype(jnp.float32)
    unit_rows = (widened * lax.rsqrt(lax.optimization_barrier(jnp.sum(widened * widened, axis=1, keepdims=True)) + epsilon)).astype(jnp.bfloat16)
    starts = (jnp.cumsum(cluster_size) - cluster_size).astype(jnp.int32)
    position = (starts[cluster_id] + cluster_rank).astype(jnp.int32)
    ordered = jnp.zeros_like(unit_rows).at[position].set(unit_rows)
    member = jnp.zeros((ROWS,), jnp.int32).at[position].set(cluster_id.astype(jnp.int32))
    place_index = jnp.arange(ROWS, dtype=jnp.int32)

    def one_block(block_no):
        first_row = (block_no * R_DEV).astype(jnp.int32)
        group_base = (first_row // GROUP_ROWS * GROUP_ROWS).astype(jnp.int32)
        queries = lax.dynamic_slice_in_dim(ordered, first_row, R_DEV, 0)
        query_cl = lax.dynamic_slice_in_dim(member, first_row, R_DEV, 0)
        query_pos = lax.dynamic_slice_in_dim(place_index, first_row, R_DEV, 0)
        key_rows = lax.dynamic_slice_in_dim(ordered, group_base, GROUP_ROWS, 0)
        key_cl = lax.dynamic_slice_in_dim(member, group_base, GROUP_ROWS, 0)
        key_pos = lax.dynamic_slice_in_dim(place_index, group_base, GROUP_ROWS, 0)
        scores = jnp.dot(queries, key_rows.T, preferred_element_type=jnp.float32)
        allowed = (key_cl[None, :] == query_cl[:, None]) & (key_pos[None, :] < query_pos[:, None])
        return lax.optimization_barrier(jnp.max(jnp.where(allowed, scores, -1.0), axis=1))
    ordered_best = lax.map(one_block, jnp.arange(ROWS // R_DEV, dtype=jnp.int32)).reshape(ROWS)
    return ordered_best[position]
```

```python
import functools

import jax
import jax.numpy as jnp
from jax import lax
from jax.experimental import pallas as pl
from jax.experimental.pallas import tpu as pltpu
from jax.sharding import PartitionSpec as P

MESH = pl.DeviceIdType.MESH
F32 = jnp.float32
BF16 = jnp.bfloat16

epsilon = 1e-06

DEVICES = 128
SLOTS = 16
CLASSES = 4
PER = DEVICES // CLASSES
CLASS_ROWS = PER * SLOTS
HALF = 512
MIX, UNMIX = 53, 29

NN = (((1,), (0,)), ((), ()))
NT = (((1,), (1,)), ((), ()))


def dot(a, b, dims=NN):
    return lax.dot_general(a, b, dims, preferred_element_type=F32)


def one_hot(mask):
    return jnp.where(mask, 1.0, 0.0).astype(BF16)


def iota(shape, dim):
    return lax.broadcasted_iota(jnp.int32, shape, dim)


def three_parts(x):
    first = x.astype(BF16)
    rest = x - first.astype(F32)
    second = rest.astype(BF16)
    third = (rest - second.astype(F32)).astype(BF16)
    return first, second, third


def kernel(
    embeds,
    ids,
    ranks,
    sizes,
    out,
    unit,
    send,
    recv,
    send_meta,
    recv_meta,
    place_of,
    gathered,
    blocks,
    tops,
    lows,
    others,
    answers,
    returned,
    send_sem,
    recv_sem,
    meta_send_sem,
    meta_recv_sem,
    block_send_sem,
    block_recv_sem,
    top_send_sem,
    top_recv_sem,
    answer_send_sem,
    answer_recv_sem,
):
    rows, width = embeds.shape
    src = lax.axis_index("src")
    grp = lax.axis_index("grp")
    x, y = src // 4, src % 4
    z, core = grp // 2, grp % 2

    def at_offset(step, sign):
        k = (step * MIX) % DEVICES
        dx, dy, dz, dc = k // 32, (k // 8) % 4, (k // 2) % 4, k % 2
        to_x = (x + sign * dx + 4) % 4
        to_y = (y + sign * dy + 4) % 4
        to_z = (z + sign * dz + 4) % 4
        return (to_x * 4 + to_y, to_z * 2 + (core + dc) % 2)

    barrier = pltpu.get_barrier_semaphore()

    def greet(step, carry):
        pl.semaphore_signal(barrier, inc=1, device_id=at_offset(step, 1), device_id_type=MESH)
        return carry

    lax.fori_loop(1, DEVICES, greet, 0)

    clusters = sizes.shape[1]
    size_row = sizes[...].astype(F32)
    earlier = iota((clusters, clusters), 1) < iota((clusters, clusters), 0)
    starts = jnp.sum(jnp.where(earlier, size_row, 0.0), axis=1, keepdims=True)
    mine = iota((clusters, rows), 0) == ids[...]
    start_row = jnp.sum(jnp.where(mine, starts, 0.0), axis=0, keepdims=True)
    position = start_row.astype(jnp.int32) + ranks[...]
    to_src = position >> 13
    to_grp = (position >> 10) & 7
    dx = ((to_src >> 2) - x) & 3
    dy = ((to_src & 3) - y) & 3
    dz = ((to_grp >> 1) - z) & 3
    dc = (to_grp - core) & 1
    step_row = ((dx * 32 + dy * 8 + dz * 2 + dc) * UNMIX) & (DEVICES - 1)
    to_step = one_hot(iota((DEVICES, rows), 0) == step_row)

    part = 256
    before = one_hot(iota((part, part), 0) < iota((part, part), 1))
    carry = jnp.zeros((DEVICES, 1), F32)
    slot_parts = []
    for n in range(rows // part):
        piece = to_step[:, n * part : (n + 1) * part]
        piece32 = piece.astype(F32)
        count = dot(piece, before) + carry
        slot_parts.append(jnp.sum(piece32 * count, axis=0, keepdims=True))
        carry = carry + jnp.sum(piece32, axis=1, keepdims=True)
    slot_row = jnp.concatenate(slot_parts, axis=1).astype(jnp.int32)
    index_row = step_row * SLOTS + slot_row
    lane_hot = one_hot(iota((DEVICES, rows), 0) == (index_row & (DEVICES - 1)))

    place_row = (position & (rows - 1)) + 1
    upper = to_step * (place_row >> 3).astype(F32).astype(BF16)
    lower = to_step * (place_row & 7).astype(F32).astype(BF16)
    meta = 8.0 * dot(upper, lane_hot, NT) + dot(lower, lane_hot, NT)
    send_meta[...] = meta.reshape(DEVICES, 1, DEVICES)
    recv_meta[0] = send_meta[0]

    pl.semaphore_wait(barrier, DEVICES - 1)

    def send_meta_step(step, carry):
        pltpu.make_async_remote_copy(
            src_ref=send_meta.at[step],
            dst_ref=recv_meta.at[step],
            send_sem=meta_send_sem,
            recv_sem=meta_recv_sem,
            device_id=at_offset(step, 1),
            device_id_type=MESH,
        ).start()
        return carry

    lax.fori_loop(1, DEVICES, send_meta_step, 0)

    def normalise(n, carry):
        here = pl.ds(pl.multiple_of(n * part, part), part)
        wide = embeds[here, :].astype(F32)
        total = jnp.sum(wide * wide, axis=1, keepdims=True)
        unit[here, :] = (wide * lax.rsqrt(total + epsilon)).astype(BF16)
        return carry

    lax.fori_loop(0, rows // part, normalise, 0)

    for n in range(CLASSES):
        pick = one_hot(iota((CLASS_ROWS, rows), 0) + n * CLASS_ROWS == index_row)
        packed = dot(pick, unit[...]).astype(BF16)
        send[pl.ds(n * PER, PER)] = packed.reshape(PER, SLOTS, width)
        if n == 0:
            recv[0] = send[0]

        def send_step(step, carry):
            pltpu.make_async_remote_copy(
                src_ref=send.at[step],
                dst_ref=recv.at[step],
                send_sem=send_sem.at[n],
                recv_sem=recv_sem.at[n],
                device_id=at_offset(step, 1),
                device_id_type=MESH,
            ).start()
            return carry

        lax.fori_loop(max(1, n * PER), (n + 1) * PER, send_step, 0)

    def wait_all(ref, sem, count):
        pltpu.make_async_copy(ref.at[pl.ds(1, count)], ref.at[pl.ds(1, count)], sem).wait()

    wait_all(recv_meta, meta_recv_sem, DEVICES - 1)

    got_places = jnp.sum(recv_meta[...].reshape(DEVICES // 8, 8, DEVICES), axis=1)
    got_places = got_places.astype(jnp.int32)
    for n in range(CLASSES):
        for m in range(CLASS_ROWS // DEVICES):
            line = n * (CLASS_ROWS // DEVICES) + m
            hit = iota((rows, DEVICES), 0) + 1 == got_places[line : line + 1, :]
            place_of[n, :, m * DEVICES : (m + 1) * DEVICES] = one_hot(hit)

    source_hot = jnp.zeros((DEVICES, rows), F32)
    lane_of = jnp.zeros((rows, DEVICES), F32)
    for n in range(CLASSES):
        group = one_hot(
            (iota((DEVICES, CLASS_ROWS), 1) + n * CLASS_ROWS) // SLOTS
            == iota((DEVICES, CLASS_ROWS), 0)
        )
        source_hot += dot(group, place_of[n], NT)
        for m in range(CLASS_ROWS // DEVICES):
            lane_of += place_of[n, :, m * DEVICES : (m + 1) * DEVICES].astype(F32)
    source_hot = source_hot.astype(BF16)
    lane_of = lane_of.astype(BF16)

    base = src * (8 * rows)
    after, prior = (z + 1) % 4, (z + 3) % 4
    crossed = z // 2
    prior_core = (core + crossed) % 2
    held = (z * 2, z * 2 + 1, after * 2 + core, prior * 2 + prior_core)
    for slot in range(4):
        for half in range(2):
            spot = held[slot] * rows + half * HALF
            places = (spot + base + iota((1, HALF), 1)).astype(F32)
            low = jnp.max(jnp.where(starts <= places, starts, 0.0), axis=0, keepdims=True)
            lows[slot * 2 + half] = low.astype(jnp.int32) - base
            tops[slot * 2 + half] = jnp.full((1, HALF), -1.0, F32)

    to_peer = (src, z * 2 + (core + 1) % 2)
    to_prior = (src, prior * 2 + core)
    to_after = (src, after * 2 + (core + after // 2) % 2)

    def block_copies(half):
        mine = blocks.at[core, half]
        for n, (slot, device) in enumerate(((core, to_peer), (2, to_prior), (3, to_after))):
            yield pltpu.make_async_remote_copy(
                src_ref=mine,
                dst_ref=blocks.at[slot, half],
                send_sem=block_send_sem.at[n, half],
                recv_sem=block_recv_sem.at[n, half],
                device_id=device,
                device_id_type=MESH,
            )

    for n in range(CLASSES):
        first = 1 if n == 0 else 0
        group = recv.at[pl.ds(n * PER + first, PER - first)]
        pltpu.make_async_copy(group, group, recv_sem.at[n]).wait()
        arrived = recv[pl.ds(n * PER, PER)].reshape(CLASS_ROWS, width)
        for half in range(2):
            here = pl.ds(half * HALF, HALF)
            found = dot(place_of[n, here, :], arrived)
            if n == 0:
                gathered[here, :] = found
            elif n < CLASSES - 1:
                gathered[here, :] += found
            else:
                blocks[core, half] = (gathered[here, :] + found).astype(BF16)
                for copy in block_copies(half):
                    copy.start()

    def spot_of(slot, half):
        number = z * 2 + slot
        number = jnp.where(slot == 2, held[2], number)
        number = jnp.where(slot == 3, held[3], number)
        return number * rows + half * HALF

    def score(key_slot, key_half, query_slot, query_half, same):
        products = dot(blocks[key_slot, key_half], blocks[query_slot, query_half], NT)
        line = query_slot * 2 + query_half
        key_no = iota((HALF, HALF), 0)
        allowed = key_no >= lows[line] - spot_of(key_slot, key_half)
        if same:
            allowed = allowed & (key_no < iota((HALF, HALF), 1))
        found = jnp.max(jnp.where(allowed, products, -1.0), axis=0, keepdims=True)
        tops[line] = jnp.maximum(tops[line], found)

    def score_pair(slot_a, half_a, slot_b, half_b):
        a_first = spot_of(slot_a, half_a) < spot_of(slot_b, half_b)
        key_slot = jnp.where(a_first, slot_a, slot_b)
        key_half = jnp.where(a_first, half_a, half_b)
        query_slot = jnp.where(a_first, slot_b, slot_a)
        query_half = jnp.where(a_first, half_b, half_a)
        score(key_slot, key_half, query_slot, query_half, False)

    def own_step(half, carry):
        score(core, half, core, half, True)
        return carry

    lax.fori_loop(0, 2, own_step, 0)

    def wait_block(n, half):
        list(block_copies(half))[n].wait_recv()

    for half in range(2):
        wait_block(0, half)

    def own_pairs(n, carry):
        plain = n == 2
        key_slot = jnp.where(plain, core, 0)
        key_half = jnp.where(plain, 0, n)
        query_slot = jnp.where(plain, core, 1)
        query_half = jnp.where(plain, 1, core)
        score(key_slot, key_half, query_slot, query_half, False)
        return carry

    lax.fori_loop(0, 3, own_pairs, 0)

    for half in range(2):
        wait_block(1, half)

        def with_after(n, carry):
            score_pair(n // 2, n % 2, 2, half)
            return carry

        lax.fori_loop(0, 4, with_after, 0)
        wait_block(2, half)

        def across(n, carry):
            number = n + half
            score_pair(3, number // 2, 2, number % 2)
            return carry

        lax.fori_loop(0, 1 + 2 * half, across, 0)

    back_prior = (src, prior * 2 + prior_core)
    back_after = (src, after * 2 + core)
    top_copies = []
    for n, (slot, device) in enumerate(
        (((core + 1) % 2, to_peer), (2, back_after), (3, back_prior))
    ):
        copy = pltpu.make_async_remote_copy(
            src_ref=tops.at[pl.ds(slot * 2, 2)],
            dst_ref=others.at[n],
            send_sem=top_send_sem.at[n],
            recv_sem=top_recv_sem.at[n],
            device_id=device,
            device_id_type=MESH,
        )
        copy.start()
        top_copies.append(copy)
    for copy in top_copies:
        copy.wait()
    halves = []
    for half in range(2):
        found = tops[core * 2 + half]
        for n in range(3):
            found = jnp.maximum(found, others[n, half])
        halves.append(found)
    best = jnp.concatenate(halves, axis=1)

    answer = jnp.zeros((DEVICES, DEVICES), F32)
    for piece in three_parts(best):
        answer += dot(source_hot * piece, lane_of)
    answers[...] = answer.reshape(DEVICES, 1, DEVICES)
    returned[0] = answers[0]

    def answer_step(step, carry):
        pltpu.make_async_remote_copy(
            src_ref=answers.at[step],
            dst_ref=returned.at[step],
            send_sem=answer_send_sem,
            recv_sem=answer_recv_sem,
            device_id=at_offset(step, -1),
            device_id_type=MESH,
        ).start()
        return carry

    lax.fori_loop(1, DEVICES, answer_step, 0)
    wait_all(returned, answer_recv_sem, DEVICES - 1)
    table = returned[...].reshape(DEVICES, DEVICES).T
    chosen = jnp.zeros((DEVICES, rows), F32)
    for piece in three_parts(table):
        chosen += dot(piece, to_step)
    out[...] = jnp.sum(chosen * lane_hot.astype(F32), axis=0, keepdims=True)

    wait_all(send_meta, meta_send_sem, DEVICES - 1)
    wait_all(answers, answer_send_sem, DEVICES - 1)
    for n in range(CLASSES):
        first = 1 if n == 0 else 0
        group = send.at[pl.ds(n * PER + first, PER - first)]
        pltpu.make_async_copy(group, group, send_sem.at[n]).wait()
    for half in range(2):
        for copy in block_copies(half):
            copy.wait_send()


def on_device(embeds, cluster_id, cluster_rank, cluster_size):
    rows, width = embeds.shape
    vmem = pl.BlockSpec(memory_space=pltpu.VMEM)
    best = pl.pallas_call(
        kernel,
        out_shape=jax.ShapeDtypeStruct((1, rows), F32),
        in_specs=[vmem] * 4,
        out_specs=vmem,
        scratch_shapes=[
            pltpu.VMEM((rows, width), BF16),
            pltpu.VMEM((DEVICES, SLOTS, width), BF16),
            pltpu.VMEM((DEVICES, SLOTS, width), BF16),
            pltpu.VMEM((DEVICES, 1, DEVICES), F32),
            pltpu.VMEM((DEVICES, 1, DEVICES), F32),
            pltpu.VMEM((CLASSES, rows, CLASS_ROWS), BF16),
            pltpu.VMEM((rows, width), F32),
            pltpu.VMEM((4, 2, HALF, width), BF16),
            pltpu.VMEM((8, 1, HALF), F32),
            pltpu.VMEM((8, 1, HALF), jnp.int32),
            pltpu.VMEM((3, 2, 1, HALF), F32),
            pltpu.VMEM((DEVICES, 1, DEVICES), F32),
            pltpu.VMEM((DEVICES, 1, DEVICES), F32),
            pltpu.SemaphoreType.DMA((CLASSES,)),
            pltpu.SemaphoreType.DMA((CLASSES,)),
            pltpu.SemaphoreType.DMA,
            pltpu.SemaphoreType.DMA,
            pltpu.SemaphoreType.DMA((3, 2)),
            pltpu.SemaphoreType.DMA((3, 2)),
            pltpu.SemaphoreType.DMA((3,)),
            pltpu.SemaphoreType.DMA((3,)),
            pltpu.SemaphoreType.DMA,
            pltpu.SemaphoreType.DMA,
        ],
        compiler_params=pltpu.CompilerParams(
            collective_id=0, has_side_effects=True, vmem_limit_bytes=50 * 1024 * 1024
        ),
        name="dedup",
    )(
        embeds,
        cluster_id.reshape(1, rows),
        cluster_rank.reshape(1, rows),
        cluster_size.reshape(1, -1),
    )
    return best.reshape(rows)


def solution(mesh):
    placed = (P(("src", "grp"), None), P(("src", "grp")), P(("src", "grp")), P())
    return jax.shard_map(
        on_device, mesh=mesh, in_specs=placed, out_specs=P(("src", "grp")), check_vma=False
    )
```

```python
import functools

import jax
import jax.numpy as jnp
from jax import lax
from jax.experimental import pallas as pl
from jax.experimental.pallas import tpu as pltpu
from jax.sharding import PartitionSpec as P

MESH = pl.DeviceIdType.MESH
F32 = jnp.float32
BF16 = jnp.bfloat16

epsilon = 1e-06

DEVICES = 128
SRC = 16
GRP = 8
LANES = 128
SLOTS = 16
CLASSES = 4
PER = DEVICES // CLASSES
CLASS_ROWS = PER * SLOTS
HALF = 512
MIX, UNMIX = 53, 29

NN = (((1,), (0,)), ((), ()))
NT = (((1,), (1,)), ((), ()))


def dot(a, b, dims=NN):
    return lax.dot_general(a, b, dims, preferred_element_type=F32)


def one_hot(mask):
    return jnp.where(mask, 1.0, 0.0).astype(BF16)


def iota(shape, dim):
    return lax.broadcasted_iota(jnp.int32, shape, dim)


def three_parts(x):
    first = x.astype(BF16)
    rest = x - first.astype(F32)
    second = rest.astype(BF16)
    third = (rest - second.astype(F32)).astype(BF16)
    return first, second, third


def kernel(
    embeds_hbm,
    ids_hbm,
    ranks_hbm,
    sizes_hbm,
    out,
    embeds,
    ids,
    ranks,
    sizes,
    unit,
    send,
    recv,
    sent_meta,
    column_meta,
    group_meta,
    place_of,
    look,
    gathered,
    blocks,
    tops,
    lows,
    others,
    best,
    answers,
    returned,
    load_sem,
    again_sem,
    send_sem,
    recv_sem,
    column_send_sem,
    column_recv_sem,
    group_send_sem,
    group_recv_sem,
    block_send_sem,
    block_recv_sem,
    top_send_sem,
    top_recv_sem,
    answer_send_sem,
    answer_recv_sem,
):
    rows, width = embeds.shape
    src = lax.axis_index("src")
    grp = lax.axis_index("grp")
    x, y = src // 4, src % 4
    z, core = grp // 2, grp % 2

    def src_at(n, sign):
        return (x + sign * (n // 4) + 4) % 4 * 4 + (y + sign * (n % 4) + 4) % 4

    def grp_at(m, sign):
        return (z + sign * (m // 2) + 4) % 4 * 2 + (core + m % 2) % 2

    loads = []
    for n, (source, target) in enumerate(
        ((ids_hbm, ids), (ranks_hbm, ranks), (sizes_hbm, sizes), (embeds_hbm, embeds))
    ):
        copy = pltpu.make_async_copy(source, target, load_sem.at[n])
        copy.start()
        loads.append(copy)

    barrier = pltpu.get_barrier_semaphore()

    def greet_src(n, carry):
        pl.semaphore_signal(barrier, inc=1, device_id=(src_at(n, 1), grp), device_id_type=MESH)
        return carry

    def greet_grp(m, carry):
        pl.semaphore_signal(barrier, inc=1, device_id=(src, grp_at(m, 1)), device_id_type=MESH)
        return carry

    lax.fori_loop(1, SRC, greet_src, 0)
    lax.fori_loop(1, GRP, greet_grp, 0)

    for copy in loads[:3]:
        copy.wait()
    clusters = sizes.shape[1]
    size_row = sizes[...].astype(F32)
    earlier = iota((clusters, clusters), 1) < iota((clusters, clusters), 0)
    starts = jnp.sum(jnp.where(earlier, size_row, 0.0), axis=1, keepdims=True)
    mine = iota((clusters, rows), 0) == ids[...]
    start_row = jnp.sum(jnp.where(mine, starts, 0.0), axis=0, keepdims=True)
    position = start_row.astype(jnp.int32) + ranks[...]
    to_src = position >> 13
    to_grp = (position >> 10) & 7
    dx = ((to_src >> 2) - x) & 3
    dy = ((to_src & 3) - y) & 3
    dz = ((to_grp >> 1) - z) & 3
    dc = (to_grp - core) & 1
    column_row = dx * 4 + dy
    step_row = ((column_row * GRP + dz * 2 + dc) * UNMIX) & (DEVICES - 1)
    to_step = one_hot(iota((DEVICES, rows), 0) == step_row)
    to_column = one_hot(iota((SRC, rows), 0) == column_row)

    part = 256
    before = one_hot(iota((part, part), 0) < iota((part, part), 1))
    carry = jnp.zeros((DEVICES, 1), F32)
    slot_parts = []
    for n in range(rows // part):
        piece = to_step[:, n * part : (n + 1) * part]
        piece32 = piece.astype(F32)
        count = dot(piece, before) + carry
        slot_parts.append(jnp.sum(piece32 * count, axis=0, keepdims=True))
        carry = carry + jnp.sum(piece32, axis=1, keepdims=True)
    slot_row = jnp.concatenate(slot_parts, axis=1).astype(jnp.int32)
    index_row = step_row * SLOTS + slot_row
    lane_hot = one_hot(iota((LANES, rows), 0) == to_grp * SLOTS + slot_row)

    place_row = (position & (rows - 1)) + 1
    upper = to_column * (place_row >> 3).astype(F32).astype(BF16)
    lower = to_column * (place_row & 7).astype(F32).astype(BF16)
    meta = 8.0 * dot(upper, lane_hot, NT) + dot(lower, lane_hot, NT)
    for n in range(SRC):
        sent_meta[n] = meta[n : n + 1, :]
    column_meta[0] = sent_meta[0]

    pl.semaphore_wait(barrier, SRC - 1 + GRP - 1)

    def greet_again(n, carry):
        pl.semaphore_signal(again_sem, inc=1, device_id=(src_at(n, 1), grp), device_id_type=MESH)
        return carry

    lax.fori_loop(1, SRC, greet_again, 0)

    def send_column_meta(n, carry):
        pltpu.make_async_remote_copy(
            src_ref=sent_meta.at[n],
            dst_ref=column_meta.at[n],
            send_sem=column_send_sem,
            recv_sem=column_recv_sem,
            device_id=(src_at(n, 1), grp),
            device_id_type=MESH,
        ).start()
        return carry

    lax.fori_loop(1, SRC, send_column_meta, 0)

    loads[3].wait()

    def normalise(n, carry):
        here = pl.ds(pl.multiple_of(n * part, part), part)
        wide = embeds[here, :].astype(F32)
        total = jnp.sum(wide * wide, axis=1, keepdims=True)
        unit[here, :] = (wide * lax.rsqrt(total + epsilon)).astype(BF16)
        return carry

    lax.fori_loop(0, rows // part, normalise, 0)

    def wait_all(ref, sem, count):
        pltpu.make_async_copy(ref.at[pl.ds(1, count)], ref.at[pl.ds(1, count)], sem).wait()

    for n in range(CLASSES):
        pick = one_hot(iota((CLASS_ROWS, rows), 0) + n * CLASS_ROWS == index_row)
        packed = dot(pick, unit[...]).astype(BF16)
        send[pl.ds(n * PER, PER)] = packed.reshape(PER, SLOTS, width)
        if n == 0:
            recv[0] = send[0]
            pl.semaphore_wait(again_sem, SRC - 1)

        def send_step(step, carry):
            k = (step * MIX) % DEVICES
            pltpu.make_async_remote_copy(
                src_ref=send.at[step],
                dst_ref=recv.at[step],
                send_sem=send_sem.at[n],
                recv_sem=recv_sem.at[n],
                device_id=(src_at(k // GRP, 1), grp_at(k % GRP, 1)),
                device_id_type=MESH,
            ).start()
            return carry

        lax.fori_loop(max(1, n * PER), (n + 1) * PER, send_step, 0)

        if n == 0:
            wait_all(column_meta, column_recv_sem, SRC - 1)
            group_meta[0] = column_meta[...]

            def send_group_meta(m, carry):
                pltpu.make_async_remote_copy(
                    src_ref=column_meta,
                    dst_ref=group_meta.at[m],
                    send_sem=group_send_sem,
                    recv_sem=group_recv_sem,
                    device_id=(src, grp_at(m, 1)),
                    device_id_type=MESH,
                ).start()
                return carry

            lax.fori_loop(1, GRP, send_group_meta, 0)

    lane_no = iota((1, LANES), 1)
    pick_rows = []
    for n in range(SRC):
        wanted = column_meta[n].astype(jnp.int32) - 1
        look[:, n * LANES : (n + 1) * LANES] = one_hot(iota((LANES, LANES), 0) == (wanted & 127))
        row_no = (lane_no // SLOTS) * 8 + (wanted >> 7)
        pick_rows.append(jnp.where(wanted >= 0, row_no, -1))
    pick_row = jnp.concatenate(pick_rows, axis=1)

    wait_all(group_meta, group_recv_sem, GRP - 1)

    all_meta = group_meta[...].reshape(DEVICES, LANES).astype(jnp.int32)
    choose = one_hot(iota((LANES, LANES), 0) == grp * SLOTS + (iota((LANES, LANES), 1) & 15))
    number = iota((DEVICES, LANES), 0)
    step_of = (((number & 15) * GRP + (number >> 4)) * UNMIX) & (DEVICES - 1)
    kept = (iota((DEVICES, LANES), 1) >> 4) == (step_of & 7)
    number = iota((SRC, DEVICES), 1)
    step_of = (((number & 15) * GRP + (number >> 4)) * UNMIX) & (DEVICES - 1)
    line_hot = one_hot((step_of >> 3) == iota((SRC, DEVICES), 0))
    got_places = jnp.zeros((SRC, LANES), F32)
    for scale, digit in ((8.0, all_meta >> 3), (1.0, all_meta & 7)):
        spread = dot(digit.astype(F32).astype(BF16), choose)
        spread = jnp.where(kept, spread, 0.0).astype(BF16)
        got_places += scale * dot(line_hot, spread)
    got_places = got_places.astype(jnp.int32)

    for n in range(CLASSES):
        for m in range(CLASS_ROWS // LANES):
            line = n * (CLASS_ROWS // LANES) + m
            hit = iota((rows, LANES), 0) + 1 == got_places[line : line + 1, :]
            place_of[n, :, m * LANES : (m + 1) * LANES] = one_hot(hit)

    base = src * (GRP * rows)
    after, prior = (z + 1) % 4, (z + 3) % 4
    prior_core = (core + z // 2) % 2

    for half_no in range(2 * GRP):
        places = (half_no * HALF + base + iota((1, HALF), 1)).astype(F32)
        low = jnp.max(jnp.where(starts <= places, starts, 0.0), axis=0, keepdims=True)
        lows[half_no] = low.astype(jnp.int32) - base
        tops[half_no] = jnp.full((1, HALF), -1.0, F32)

    to_peer = (src, z * 2 + (core + 1) % 2)
    to_prior = (src, prior * 2 + core)
    to_after = (src, after * 2 + (core + after // 2) % 2)

    def block_copies(half):
        mine = blocks.at[core, half]
        for n, (slot, device) in enumerate(((core, to_peer), (2, to_prior), (3, to_after))):
            yield pltpu.make_async_remote_copy(
                src_ref=mine,
                dst_ref=blocks.at[slot, half],
                send_sem=block_send_sem.at[n, half],
                recv_sem=block_recv_sem.at[n, half],
                device_id=device,
                device_id_type=MESH,
            )

    for n in range(CLASSES):
        first = 1 if n == 0 else 0
        group = recv.at[pl.ds(n * PER + first, PER - first)]
        pltpu.make_async_copy(group, group, recv_sem.at[n]).wait()
        arrived = recv[pl.ds(n * PER, PER)].reshape(CLASS_ROWS, width)
        for half in range(2):
            here = pl.ds(half * HALF, HALF)
            found = dot(place_of[n, here, :], arrived)
            if n == 0:
                gathered[here, :] = found
            elif n < CLASSES - 1:
                gathered[here, :] += found
            else:
                blocks[core, half] = (gathered[here, :] + found).astype(BF16)
                for copy in block_copies(half):
                    copy.start()

    def half_of(slot, half):
        block_no = z * 2 + slot
        block_no = jnp.where(slot == 2, after * 2 + core, block_no)
        block_no = jnp.where(slot == 3, prior * 2 + prior_core, block_no)
        return block_no * 2 + half

    def score(key_slot, key_half, query_slot, query_half, same):
        products = dot(blocks[key_slot, key_half], blocks[query_slot, query_half], NT)
        line = half_of(query_slot, query_half)
        key_no = iota((HALF, HALF), 0)
        allowed = key_no >= lows[line] - half_of(key_slot, key_half) * HALF
        if same:
            allowed = allowed & (key_no < iota((HALF, HALF), 1))
        found = jnp.max(jnp.where(allowed, products, -1.0), axis=0, keepdims=True)
        tops[line] = jnp.maximum(tops[line], found)

    def score_pair(slot_a, half_a, slot_b, half_b):
        a_first = half_of(slot_a, half_a) < half_of(slot_b, half_b)
        key_slot = jnp.where(a_first, slot_a, slot_b)
        key_half = jnp.where(a_first, half_a, half_b)
        query_slot = jnp.where(a_first, slot_b, slot_a)
        query_half = jnp.where(a_first, half_b, half_a)
        score(key_slot, key_half, query_slot, query_half, False)

    def own_step(half, carry):
        score(core, half, core, half, True)
        return carry

    lax.fori_loop(0, 2, own_step, 0)

    def wait_block(n, half):
        slot = ((core + 1) % 2, 2, 3)[n]
        here = blocks.at[slot, half]
        pltpu.make_async_copy(here, here, block_recv_sem.at[n, half]).wait()

    for half in range(2):
        wait_block(0, half)

    def own_pairs(n, carry):
        plain = n == 2
        key_slot = jnp.where(plain, core, 0)
        key_half = jnp.where(plain, 0, n)
        query_slot = jnp.where(plain, core, 1)
        query_half = jnp.where(plain, 1, core)
        score(key_slot, key_half, query_slot, query_half, False)
        return carry

    lax.fori_loop(0, 3, own_pairs, 0)

    for half in range(2):
        wait_block(1, half)

        def with_after(n, carry):
            score_pair(n // 2, n % 2, 2, half)
            return carry

        lax.fori_loop(0, 4, with_after, 0)
        wait_block(2, half)

        def across(n, carry):
            number = n + half
            score_pair(3, number // 2, 2, number % 2)
            return carry

        lax.fori_loop(0, 1 + 2 * half, across, 0)

    def send_tops(m, carry):
        pltpu.make_async_remote_copy(
            src_ref=tops,
            dst_ref=others.at[m],
            send_sem=top_send_sem,
            recv_sem=top_recv_sem,
            device_id=(src, grp_at(m, 1)),
            device_id_type=MESH,
        ).start()
        return carry

    lax.fori_loop(1, GRP, send_tops, 0)
    wait_all(others, top_recv_sem, GRP - 1)
    for half_no in range(2 * GRP):
        found = tops[half_no]
        for m in range(1, GRP):
            found = jnp.maximum(found, others[m, half_no])
        for n in range(HALF // LANES):
            line = half_no * (HALF // LANES) + n
            best[line : line + 1, :] = found[:, n * LANES : (n + 1) * LANES]

    answer = jnp.zeros((best.shape[0], SRC * LANES), F32)
    for piece in three_parts(best[...]):
        answer += dot(piece, look[...])
    right = iota(answer.shape, 0) == pick_row
    answer = jnp.sum(jnp.where(right, answer, 0.0), axis=0, keepdims=True)
    for n in range(SRC):
        answers[n] = answer[:, n * LANES : (n + 1) * LANES]
    returned[0] = answers[0]

    def send_answer(n, carry):
        pltpu.make_async_remote_copy(
            src_ref=answers.at[n],
            dst_ref=returned.at[n],
            send_sem=answer_send_sem,
            recv_sem=answer_recv_sem,
            device_id=(src_at(n, -1), grp),
            device_id_type=MESH,
        ).start()
        return carry

    lax.fori_loop(1, SRC, send_answer, 0)
    wait_all(returned, answer_recv_sem, SRC - 1)
    table = returned[...].reshape(SRC, LANES).T
    chosen = jnp.zeros((LANES, rows), F32)
    for piece in three_parts(table):
        chosen += dot(piece, to_column)
    out[...] = jnp.sum(chosen * lane_hot.astype(F32), axis=0, keepdims=True)

    wait_all(sent_meta, column_send_sem, SRC - 1)
    wait_all(group_meta, group_send_sem, GRP - 1)
    wait_all(others, top_send_sem, GRP - 1)
    wait_all(answers, answer_send_sem, SRC - 1)
    for n in range(CLASSES):
        first = 1 if n == 0 else 0
        group = send.at[pl.ds(n * PER + first, PER - first)]
        pltpu.make_async_copy(group, group, send_sem.at[n]).wait()
    for n in range(3):
        for half in range(2):
            here = blocks.at[core, half]
            pltpu.make_async_copy(here, here, block_send_sem.at[n, half]).wait()


def on_device(embeds, cluster_id, cluster_rank, cluster_size):
    rows, width = embeds.shape
    clusters = cluster_size.shape[0]
    best = pl.pallas_call(
        kernel,
        out_shape=jax.ShapeDtypeStruct((1, rows), F32),
        in_specs=[pl.BlockSpec(memory_space=pl.ANY)] * 4,
        out_specs=pl.BlockSpec(memory_space=pltpu.VMEM),
        scratch_shapes=[
            pltpu.VMEM((rows, width), BF16),
            pltpu.VMEM((1, rows), jnp.int32),
            pltpu.VMEM((1, rows), jnp.int32),
            pltpu.VMEM((1, clusters), jnp.int32),
            pltpu.VMEM((rows, width), BF16),
            pltpu.VMEM((DEVICES, SLOTS, width), BF16),
            pltpu.VMEM((DEVICES, SLOTS, width), BF16),
            pltpu.VMEM((SRC, 1, LANES), F32),
            pltpu.VMEM((SRC, 1, LANES), F32),
            pltpu.VMEM((GRP, SRC, 1, LANES), F32),
            pltpu.VMEM((CLASSES, rows, CLASS_ROWS), BF16),
            pltpu.VMEM((LANES, SRC * LANES), BF16),
            pltpu.VMEM((rows, width), F32),
            pltpu.VMEM((4, 2, HALF, width), BF16),
            pltpu.VMEM((2 * GRP, 1, HALF), F32),
            pltpu.VMEM((2 * GRP, 1, HALF), jnp.int32),
            pltpu.VMEM((GRP, 2 * GRP, 1, HALF), F32),
            pltpu.VMEM((GRP * rows // LANES, LANES), F32),
            pltpu.VMEM((SRC, 1, LANES), F32),
            pltpu.VMEM((SRC, 1, LANES), F32),
            pltpu.SemaphoreType.DMA((4,)),
            pltpu.SemaphoreType.REGULAR,
            pltpu.SemaphoreType.DMA((CLASSES,)),
            pltpu.SemaphoreType.DMA((CLASSES,)),
            pltpu.SemaphoreType.DMA,
            pltpu.SemaphoreType.DMA,
            pltpu.SemaphoreType.DMA,
            pltpu.SemaphoreType.DMA,
            pltpu.SemaphoreType.DMA((3, 2)),
            pltpu.SemaphoreType.DMA((3, 2)),
            pltpu.SemaphoreType.DMA,
            pltpu.SemaphoreType.DMA,
            pltpu.SemaphoreType.DMA,
            pltpu.SemaphoreType.DMA,
        ],
        compiler_params=pltpu.CompilerParams(
            collective_id=0, has_side_effects=True, vmem_limit_bytes=50 * 1024 * 1024
        ),
        name="dedup",
    )(
        embeds,
        cluster_id.reshape(1, rows),
        cluster_rank.reshape(1, rows),
        cluster_size.reshape(1, -1),
    )
    return best.reshape(rows)


def solution(mesh):
    placed = (P(("src", "grp"), None), P(("src", "grp")), P(("src", "grp")), P())
    return jax.shard_map(
        on_device, mesh=mesh, in_specs=placed, out_specs=P(("src", "grp")), check_vma=False
    )
```

```python
import jax
import jax.numpy as jnp
from jax import lax
from jax.experimental import pallas as pl
from jax.experimental.pallas import tpu as pltpu
from jax.sharding import PartitionSpec as P

MESH = pl.DeviceIdType.MESH
F32 = jnp.float32
BF16 = jnp.bfloat16

epsilon = 1e-06

DEVICES = 128
SRC = 16
GRP = 8
LANES = 128
SLOTS = 16
CLASSES = 4
PER = DEVICES // CLASSES
CLASS_ROWS = PER * SLOTS
HALF = 512
QUARTER = 256
HELD = 6
MIX, UNMIX = 53, 29

NN = (((1,), (0,)), ((), ()))
NT = (((1,), (1,)), ((), ()))


def dot(a, b, dims=NN):
    return lax.dot_general(a, b, dims, preferred_element_type=F32)


def one_hot(mask):
    return jnp.where(mask, 1.0, 0.0).astype(BF16)


def iota(shape, dim):
    return lax.broadcasted_iota(jnp.int32, shape, dim)


def three_parts(x):
    first = x.astype(BF16)
    rest = x - first.astype(F32)
    second = rest.astype(BF16)
    third = (rest - second.astype(F32)).astype(BF16)
    return first, second, third


def kernel(
    embeds_hbm,
    ids_hbm,
    ranks_hbm,
    sizes_hbm,
    out,
    embeds,
    ids,
    ranks,
    sizes,
    unit,
    send,
    recv,
    sent_meta,
    column_meta,
    group_meta,
    place_of,
    look,
    gathered,
    blocks,
    tops,
    lows,
    others,
    own_best,
    best,
    answers,
    returned,
    load_sem,
    again_sem,
    send_sem,
    recv_sem,
    column_send_sem,
    column_recv_sem,
    group_send_sem,
    group_recv_sem,
    block_send_sem,
    block_recv_sem,
    peer_send_sem,
    peer_recv_sem,
    forward_send_sem,
    forward_recv_sem,
    top_send_sem,
    top_recv_sem,
    best_send_sem,
    best_recv_sem,
    answer_send_sem,
    answer_recv_sem,
):
    rows, width = embeds.shape
    src = lax.axis_index("src")
    grp = lax.axis_index("grp")
    x, y = src // 4, src % 4
    z, core = grp // 2, grp % 2

    def src_at(n, sign):
        return (x + sign * (n // 4) + 4) % 4 * 4 + (y + sign * (n % 4) + 4) % 4

    def grp_at(m, sign):
        return (z + sign * (m // 2) + 4) % 4 * 2 + (core + m % 2) % 2

    loads = []
    for n, (source, target) in enumerate(
        ((ids_hbm, ids), (ranks_hbm, ranks), (sizes_hbm, sizes), (embeds_hbm, embeds))
    ):
        copy = pltpu.make_async_copy(source, target, load_sem.at[n])
        copy.start()
        loads.append(copy)

    barrier = pltpu.get_barrier_semaphore()

    def greet_src(n, carry):
        pl.semaphore_signal(barrier, inc=1, device_id=(src_at(n, 1), grp), device_id_type=MESH)
        return carry

    def greet_grp(m, carry):
        pl.semaphore_signal(barrier, inc=1, device_id=(src, grp_at(m, 1)), device_id_type=MESH)
        return carry

    lax.fori_loop(1, SRC, greet_src, 0)
    lax.fori_loop(1, GRP, greet_grp, 0)

    for copy in loads[:3]:
        copy.wait()
    clusters = sizes.shape[1]
    size_row = sizes[...].astype(F32)
    earlier = iota((clusters, clusters), 1) < iota((clusters, clusters), 0)
    starts = jnp.sum(jnp.where(earlier, size_row, 0.0), axis=1, keepdims=True)
    mine = iota((clusters, rows), 0) == ids[...]
    start_row = jnp.sum(jnp.where(mine, starts, 0.0), axis=0, keepdims=True)
    position = start_row.astype(jnp.int32) + ranks[...]
    tiling = position >> 16
    to_x = (((position >> 15) & 1) * 2 + ((position >> 12) & 1) - tiling) & 3
    to_y = (((position >> 14) & 1) * 2 + ((position >> 11) & 1) - tiling) & 3
    to_z = (((position >> 13) & 1) * 2 + ((position >> 10) & 1) - tiling) & 3
    to_core = (position >> 9) & 1
    to_grp = to_z * 2 + to_core
    dx, dy, dz = (to_x - x) & 3, (to_y - y) & 3, (to_z - z) & 3
    dc = (to_core - core) & 1
    column_row = dx * 4 + dy
    step_row = ((column_row * GRP + dz * 2 + dc) * UNMIX) & (DEVICES - 1)
    to_step = one_hot(iota((DEVICES, rows), 0) == step_row)
    to_column = one_hot(iota((SRC, rows), 0) == column_row)

    part = 256
    before = one_hot(iota((part, part), 0) < iota((part, part), 1))
    carry = jnp.zeros((DEVICES, 1), F32)
    slot_parts = []
    for n in range(rows // part):
        piece = to_step[:, n * part : (n + 1) * part]
        piece32 = piece.astype(F32)
        count = dot(piece, before) + carry
        slot_parts.append(jnp.sum(piece32 * count, axis=0, keepdims=True))
        carry = carry + jnp.sum(piece32, axis=1, keepdims=True)
    slot_row = jnp.concatenate(slot_parts, axis=1).astype(jnp.int32)
    index_row = step_row * SLOTS + slot_row
    lane_hot = one_hot(iota((LANES, rows), 0) == to_grp * SLOTS + slot_row)

    place_row = tiling * HALF + (position & (HALF - 1)) + 1
    upper = to_column * (place_row >> 3).astype(F32).astype(BF16)
    lower = to_column * (place_row & 7).astype(F32).astype(BF16)
    meta = 8.0 * dot(upper, lane_hot, NT) + dot(lower, lane_hot, NT)
    for n in range(SRC):
        sent_meta[n] = meta[n : n + 1, :]
    column_meta[0] = sent_meta[0]

    pl.semaphore_wait(barrier, SRC - 1 + GRP - 1)

    def greet_again(n, carry):
        pl.semaphore_signal(again_sem, inc=1, device_id=(src_at(n, 1), grp), device_id_type=MESH)
        return carry

    lax.fori_loop(1, SRC, greet_again, 0)

    def send_column_meta(n, carry):
        pltpu.make_async_remote_copy(
            src_ref=sent_meta.at[n],
            dst_ref=column_meta.at[n],
            send_sem=column_send_sem,
            recv_sem=column_recv_sem,
            device_id=(src_at(n, 1), grp),
            device_id_type=MESH,
        ).start()
        return carry

    lax.fori_loop(1, SRC, send_column_meta, 0)

    loads[3].wait()

    def normalise(n, carry):
        here = pl.ds(pl.multiple_of(n * part, part), part)
        wide = embeds[here, :].astype(F32)
        total = jnp.sum(wide * wide, axis=1, keepdims=True)
        unit[here, :] = (wide * lax.rsqrt(total + epsilon)).astype(BF16)
        return carry

    lax.fori_loop(0, rows // part, normalise, 0)

    def wait_all(ref, sem, count):
        pltpu.make_async_copy(ref.at[pl.ds(1, count)], ref.at[pl.ds(1, count)], sem).wait()

    for n in range(CLASSES):
        pick = one_hot(iota((CLASS_ROWS, rows), 0) + n * CLASS_ROWS == index_row)
        packed = dot(pick, unit[...]).astype(BF16)
        send[pl.ds(n * PER, PER)] = packed.reshape(PER, SLOTS, width)
        if n == 0:
            recv[0] = send[0]
            pl.semaphore_wait(again_sem, SRC - 1)

        def send_step(step, carry):
            k = (step * MIX) % DEVICES
            pltpu.make_async_remote_copy(
                src_ref=send.at[step],
                dst_ref=recv.at[step],
                send_sem=send_sem.at[n],
                recv_sem=recv_sem.at[n],
                device_id=(src_at(k // GRP, 1), grp_at(k % GRP, 1)),
                device_id_type=MESH,
            ).start()
            return carry

        lax.fori_loop(max(1, n * PER), (n + 1) * PER, send_step, 0)

        if n == 0:
            wait_all(column_meta, column_recv_sem, SRC - 1)
            group_meta[0] = column_meta[...]

            def send_group_meta(m, carry):
                pltpu.make_async_remote_copy(
                    src_ref=column_meta,
                    dst_ref=group_meta.at[m],
                    send_sem=group_send_sem,
                    recv_sem=group_recv_sem,
                    device_id=(src, grp_at(m, 1)),
                    device_id_type=MESH,
                ).start()
                return carry

            lax.fori_loop(1, GRP, send_group_meta, 0)

    lane_no = iota((1, LANES), 1)
    pick_rows = []
    for n in range(SRC):
        wanted = column_meta[n].astype(jnp.int32) - 1
        look[:, n * LANES : (n + 1) * LANES] = one_hot(iota((LANES, LANES), 0) == (wanted & 127))
        row_no = (lane_no // SLOTS) * 8 + (wanted >> 7)
        pick_rows.append(jnp.where(wanted >= 0, row_no, -1))
    pick_row = jnp.concatenate(pick_rows, axis=1)

    wait_all(group_meta, group_recv_sem, GRP - 1)

    all_meta = group_meta[...].reshape(DEVICES, LANES).astype(jnp.int32)
    choose = one_hot(iota((LANES, LANES), 0) == grp * SLOTS + (iota((LANES, LANES), 1) & 15))
    number = iota((DEVICES, LANES), 0)
    step_of = (((number & 15) * GRP + (number >> 4)) * UNMIX) & (DEVICES - 1)
    kept = (iota((DEVICES, LANES), 1) >> 4) == (step_of & 7)
    number = iota((SRC, DEVICES), 1)
    step_of = (((number & 15) * GRP + (number >> 4)) * UNMIX) & (DEVICES - 1)
    line_hot = one_hot((step_of >> 3) == iota((SRC, DEVICES), 0))
    got_places = jnp.zeros((SRC, LANES), F32)
    for scale, digit in ((8.0, all_meta >> 3), (1.0, all_meta & 7)):
        spread = dot(digit.astype(F32).astype(BF16), choose)
        spread = jnp.where(kept, spread, 0.0).astype(BF16)
        got_places += scale * dot(line_hot, spread)
    got_places = got_places.astype(jnp.int32)

    for n in range(CLASSES):
        for m in range(CLASS_ROWS // LANES):
            line = n * (CLASS_ROWS // LANES) + m
            hit = iota((rows, LANES), 0) + 1 == got_places[line : line + 1, :]
            place_of[n, :, m * LANES : (m + 1) * LANES] = one_hot(hit)

    def bits(tiling):
        return (x + tiling) % 2, (y + tiling) % 2, (z + tiling) % 2

    def across(tiling, *axes):
        place = [x, y, z]
        for axis in axes:
            place[axis] = (place[axis] + 1 - 2 * bits(tiling)[axis] + 4) % 4
        return place

    def device_across(tiling, axes, to_core):
        to_x, to_y, to_z = across(tiling, *axes)
        return (to_x * 4 + to_y, to_z * 2 + to_core)

    def number(tiling, slot):
        v1, v2, v3 = bits(tiling)
        if not isinstance(slot, int) or slot < 2:
            own = slot
        elif slot == 2:
            v1, own = 1 - v1, (core + v1) % 2
        elif slot == 3:
            v2, own = 1 - v2, core
        elif slot == 4:
            v3, own = 1 - v3, (core + v2) % 2
        else:
            v2, v3, own = 1 - v2, 1 - v3, core
        return ((v1 * 2 + v2) * 2 + v3) * 2 + own

    def base(tiling):
        cube_x, cube_y, cube_z = ((i + tiling) % 4 // 2 for i in (x, y, z))
        return (tiling * 8 + cube_x * 4 + cube_y * 2 + cube_z) * (GRP * rows)

    for tiling in range(2):
        for slot in range(HELD):
            places = number(tiling, slot) * HALF + base(tiling) + iota((1, HALF), 1)
            below = jnp.where(starts <= places.astype(F32), starts, 0.0)
            low = jnp.max(below, axis=0, keepdims=True)
            lows[tiling, slot] = low.astype(jnp.int32) - base(tiling)
            tops[tiling, slot] = jnp.full((1, HALF), -1.0, F32)

    def first_half(axis):
        return 1 if axis == 1 else 0

    def neighbour_copy(tiling, axis, half):
        v1, v2, v3 = bits(tiling)
        to_core = (core + (1 - v1, 0, v2)[axis]) % 2
        here = pl.ds(half * QUARTER, QUARTER)
        return pltpu.make_async_remote_copy(
            src_ref=blocks.at[tiling, core, here],
            dst_ref=blocks.at[tiling, 2 + axis, here],
            send_sem=block_send_sem.at[tiling, axis, half],
            recv_sem=block_recv_sem.at[tiling, axis, half],
            device_id=device_across(tiling, (axis,), to_core),
            device_id_type=MESH,
        )

    def peer_copy(tiling):
        return pltpu.make_async_remote_copy(
            src_ref=blocks.at[tiling, core],
            dst_ref=blocks.at[tiling, core],
            send_sem=peer_send_sem.at[tiling],
            recv_sem=peer_recv_sem.at[tiling],
            device_id=(src, z * 2 + (core + 1) % 2),
            device_id_type=MESH,
        )

    def forward_copy(tiling, axis):
        half = first_half(axis)
        here = pl.ds(half * QUARTER, QUARTER)
        to_core = core if axis == 1 else (core + bits(tiling)[1]) % 2
        return pltpu.make_async_remote_copy(
            src_ref=blocks.at[tiling, 2 + axis, here],
            dst_ref=blocks.at[tiling, 5, here],
            send_sem=forward_send_sem.at[tiling, half],
            recv_sem=forward_recv_sem.at[tiling, half],
            device_id=device_across(tiling, (3 - axis,), to_core),
            device_id_type=MESH,
        )

    for n in range(CLASSES):
        first = 1 if n == 0 else 0
        group = recv.at[pl.ds(n * PER + first, PER - first)]
        pltpu.make_async_copy(group, group, recv_sem.at[n]).wait()
        arrived = recv[pl.ds(n * PER, PER)].reshape(CLASS_ROWS, width)
        for tiling in range(2):
            here = pl.ds(tiling * HALF, HALF)
            found = dot(place_of[n, here, :], arrived)
            if n == 0:
                gathered[here, :] = found
            elif n < CLASSES - 1:
                gathered[here, :] += found
            else:
                blocks[tiling, core] = (gathered[here, :] + found).astype(BF16)
                for axis in range(3):
                    neighbour_copy(tiling, axis, first_half(axis)).start()
                peer_copy(tiling).start()
                for axis in range(3):
                    neighbour_copy(tiling, axis, 1 - first_half(axis)).start()

    def score(tiling, key, query, same=False):
        key_slot, key_start, keys = key[:3]
        query_slot, query_start, queries = query[:3]
        products = dot(
            blocks[tiling, key_slot, pl.ds(key_start, keys), :],
            blocks[tiling, query_slot, pl.ds(query_start, queries), :],
            NT,
        )
        columns = slice(query_start, query_start + queries)
        key_no = iota((keys, queries), 0) + key_start
        allowed = key_no >= lows[tiling, query_slot][:, columns] - key[3] * HALF
        if same:
            allowed = allowed & (key_no < iota((keys, queries), 1) + query_start)
        found = jnp.max(jnp.where(allowed, products, -1.0), axis=0, keepdims=True)
        tops[tiling, query_slot, :, columns] = jnp.maximum(
            tops[tiling, query_slot, :, columns], found
        )

    def pair(tiling, a, b):
        a, b = (*a, number(tiling, a[0])), (*b, number(tiling, b[0]))
        a_first = a[3] < b[3]

        @pl.when(a_first)
        def _():
            score(tiling, a, b)

        @pl.when(jnp.logical_not(a_first))
        def _():
            score(tiling, b, a)

    def own_slot(tiling, axis):
        v1, v2, v3 = bits(tiling)
        return (core + (0, v2, v2 + v3)[axis]) % 2

    def own_scores(tiling, carry):
        mine = (core, 0, HALF, number(tiling, core))
        score(tiling, mine, mine, True)
        peer = blocks.at[tiling, (core + 1) % 2]
        pltpu.make_async_copy(peer, peer, peer_recv_sem.at[tiling]).wait()
        start = pl.multiple_of(core * QUARTER, QUARTER)
        key = (0, start, QUARTER, number(tiling, 0))
        score(tiling, key, (1, 0, HALF, number(tiling, 1)))
        return carry

    lax.fori_loop(0, 2, own_scores, 0)

    def wait_neighbour(tiling, axis, half):
        here = blocks.at[tiling, 2 + axis, pl.ds(half * QUARTER, QUARTER)]
        pltpu.make_async_copy(here, here, block_recv_sem.at[tiling, axis, half]).wait()

    def forward(tiling, carry):
        for axis in (1, 2):
            wait_neighbour(tiling, axis, first_half(axis))
            forward_copy(tiling, axis).start()
        return carry

    lax.fori_loop(0, 2, forward, 0)

    def held_part(axis, half):
        return (2 + axis, half * QUARTER, QUARTER)

    def first_scores(tiling, carry):
        wait_neighbour(tiling, 0, first_half(0))
        for axis in range(3):
            own = (own_slot(tiling, axis), 0, HALF)
            pair(tiling, own, held_part(axis, first_half(axis)))
        for axis, other in ((0, 1), (0, 2), (1, 2)):
            pair(
                tiling, held_part(axis, first_half(axis)), held_part(other, first_half(other))
            )
        return carry

    lax.fori_loop(0, 2, first_scores, 0)

    def second_scores(tiling, carry):
        for axis in range(3):
            wait_neighbour(tiling, axis, 1 - first_half(axis))
            own = (own_slot(tiling, axis), 0, HALF)
            pair(tiling, own, held_part(axis, 1 - first_half(axis)))
        for axis, other in ((0, 1), (0, 2), (1, 2)):
            pair(tiling, held_part(axis, 1 - first_half(axis)), (2 + other, 0, HALF))
            pair(
                tiling,
                held_part(axis, first_half(axis)),
                held_part(other, 1 - first_half(other)),
            )
        return carry

    lax.fori_loop(0, 2, second_scores, 0)

    def far_scores(tiling, carry):
        for half in range(2):
            here = blocks.at[tiling, 5, pl.ds(half * QUARTER, QUARTER)]
            pltpu.make_async_copy(here, here, forward_recv_sem.at[tiling, half]).wait()
            pair(tiling, (2, 0, HALF), (5, half * QUARTER, QUARTER))
        return carry

    lax.fori_loop(0, 2, far_scores, 0)

    for tiling in range(2):
        v1, v2, v3 = bits(tiling)
        targets = (
            ((core + 1) % 2, (), (core + 1) % 2),
            (2, (0,), (core + v1) % 2),
            (3, (1,), core),
            (4, (2,), (core + v2) % 2),
            (5, (1, 2), core),
        )
        for n, (slot, axes, to_core) in enumerate(targets):
            pltpu.make_async_remote_copy(
                src_ref=tops.at[tiling, slot],
                dst_ref=others.at[tiling * 5 + n],
                send_sem=top_send_sem,
                recv_sem=top_recv_sem,
                device_id=device_across(tiling, axes, to_core),
                device_id_type=MESH,
            ).start()
    pltpu.make_async_copy(others, others, top_recv_sem).wait()
    for tiling in range(2):
        found = tops[tiling, core]
        for n in range(5):
            found = jnp.maximum(found, others[tiling * 5 + n])
        for n in range(HALF // LANES):
            line = tiling * (HALF // LANES) + n
            own_best[line : line + 1, :] = found[:, n * LANES : (n + 1) * LANES]

    best[grp] = own_best[...]

    def send_best(m, carry):
        pltpu.make_async_remote_copy(
            src_ref=own_best,
            dst_ref=best.at[grp],
            send_sem=best_send_sem,
            recv_sem=best_recv_sem,
            device_id=(src, grp_at(m, 1)),
            device_id_type=MESH,
        ).start()
        return carry

    lax.fori_loop(1, GRP, send_best, 0)
    wait_all(best, best_recv_sem, GRP - 1)

    answer = jnp.zeros((GRP * rows // LANES, SRC * LANES), F32)
    for piece in three_parts(best[...].reshape(GRP * rows // LANES, LANES)):
        answer += dot(piece, look[...])
    right = iota(answer.shape, 0) == pick_row
    answer = jnp.sum(jnp.where(right, answer, 0.0), axis=0, keepdims=True)
    for n in range(SRC):
        answers[n] = answer[:, n * LANES : (n + 1) * LANES]
    returned[0] = answers[0]

    def send_answer(n, carry):
        pltpu.make_async_remote_copy(
            src_ref=answers.at[n],
            dst_ref=returned.at[n],
            send_sem=answer_send_sem,
            recv_sem=answer_recv_sem,
            device_id=(src_at(n, -1), grp),
            device_id_type=MESH,
        ).start()
        return carry

    lax.fori_loop(1, SRC, send_answer, 0)
    wait_all(returned, answer_recv_sem, SRC - 1)
    table = returned[...].reshape(SRC, LANES).T
    chosen = jnp.zeros((LANES, rows), F32)
    for piece in three_parts(table):
        chosen += dot(piece, to_column)
    out[...] = jnp.sum(chosen * lane_hot.astype(F32), axis=0, keepdims=True)

    wait_all(sent_meta, column_send_sem, SRC - 1)
    wait_all(group_meta, group_send_sem, GRP - 1)
    pltpu.make_async_copy(others, others, top_send_sem).wait()
    wait_all(best, best_send_sem, GRP - 1)
    wait_all(answers, answer_send_sem, SRC - 1)
    for n in range(CLASSES):
        first = 1 if n == 0 else 0
        group = send.at[pl.ds(n * PER + first, PER - first)]
        pltpu.make_async_copy(group, group, send_sem.at[n]).wait()
    for tiling in range(2):
        whole = blocks.at[tiling, core]
        pltpu.make_async_copy(whole, whole, peer_send_sem.at[tiling]).wait()
        for half in range(2):
            here = blocks.at[tiling, core, pl.ds(half * QUARTER, QUARTER)]
            for axis in range(3):
                pltpu.make_async_copy(here, here, block_send_sem.at[tiling, axis, half]).wait()
            pltpu.make_async_copy(here, here, forward_send_sem.at[tiling, half]).wait()


def on_device(embeds, cluster_id, cluster_rank, cluster_size):
    rows, width = embeds.shape
    clusters = cluster_size.shape[0]
    best = pl.pallas_call(
        kernel,
        out_shape=jax.ShapeDtypeStruct((1, rows), F32),
        in_specs=[pl.BlockSpec(memory_space=pl.ANY)] * 4,
        out_specs=pl.BlockSpec(memory_space=pltpu.VMEM),
        scratch_shapes=[
            pltpu.VMEM((rows, width), BF16),
            pltpu.VMEM((1, rows), jnp.int32),
            pltpu.VMEM((1, rows), jnp.int32),
            pltpu.VMEM((1, clusters), jnp.int32),
            pltpu.VMEM((rows, width), BF16),
            pltpu.VMEM((DEVICES, SLOTS, width), BF16),
            pltpu.VMEM((DEVICES, SLOTS, width), BF16),
            pltpu.VMEM((SRC, 1, LANES), F32),
            pltpu.VMEM((SRC, 1, LANES), F32),
            pltpu.VMEM((GRP, SRC, 1, LANES), F32),
            pltpu.VMEM((CLASSES, rows, CLASS_ROWS), BF16),
            pltpu.VMEM((LANES, SRC * LANES), BF16),
            pltpu.VMEM((rows, width), F32),
            pltpu.VMEM((2, HELD, HALF, width), BF16),
            pltpu.VMEM((2, HELD, 1, HALF), F32),
            pltpu.VMEM((2, HELD, 1, HALF), jnp.int32),
            pltpu.VMEM((2 * (HELD - 1), 1, HALF), F32),
            pltpu.VMEM((rows // LANES, LANES), F32),
            pltpu.VMEM((GRP, rows // LANES, LANES), F32),
            pltpu.VMEM((SRC, 1, LANES), F32),
            pltpu.VMEM((SRC, 1, LANES), F32),
            pltpu.SemaphoreType.DMA((4,)),
            pltpu.SemaphoreType.REGULAR,
            pltpu.SemaphoreType.DMA((CLASSES,)),
            pltpu.SemaphoreType.DMA((CLASSES,)),
            pltpu.SemaphoreType.DMA,
            pltpu.SemaphoreType.DMA,
            pltpu.SemaphoreType.DMA,
            pltpu.SemaphoreType.DMA,
            pltpu.SemaphoreType.DMA((2, 3, 2)),
            pltpu.SemaphoreType.DMA((2, 3, 2)),
            pltpu.SemaphoreType.DMA((2,)),
            pltpu.SemaphoreType.DMA((2,)),
            pltpu.SemaphoreType.DMA((2, 2)),
            pltpu.SemaphoreType.DMA((2, 2)),
            pltpu.SemaphoreType.DMA,
            pltpu.SemaphoreType.DMA,
            pltpu.SemaphoreType.DMA,
            pltpu.SemaphoreType.DMA,
            pltpu.SemaphoreType.DMA,
            pltpu.SemaphoreType.DMA,
        ],
        compiler_params=pltpu.CompilerParams(
            collective_id=0, has_side_effects=True, vmem_limit_bytes=50 * 1024 * 1024
        ),
        name="dedup",
    )(
        embeds,
        cluster_id.reshape(1, rows),
        cluster_rank.reshape(1, rows),
        cluster_size.reshape(1, -1),
    )
    return best.reshape(rows)


def solution(mesh):
    placed = (P(("src", "grp"), None), P(("src", "grp")), P(("src", "grp")), P())
    return jax.shard_map(
        on_device, mesh=mesh, in_specs=placed, out_specs=P(("src", "grp")), check_vma=False
    )
```

```python
import jax
import jax.numpy as jnp
from jax import lax
from jax.experimental import pallas as pl
from jax.experimental.pallas import tpu as pltpu
from jax.sharding import PartitionSpec as P

MESH = pl.DeviceIdType.MESH
F32 = jnp.float32
BF16 = jnp.bfloat16

epsilon = 1e-06

DEVICES = 128
SRC = 16
GRP = 8
LANES = 128
SLOTS = 16
CLASSES = 4
PER = DEVICES // CLASSES
CLASS_ROWS = PER * SLOTS
HALF = 512
QUARTER = 256
HELD = 6
EARLY = 58
MIX, UNMIX = 53, 29

NN = (((1,), (0,)), ((), ()))
NT = (((1,), (1,)), ((), ()))


def dot(a, b, dims=NN):
    return lax.dot_general(a, b, dims, preferred_element_type=F32)


def one_hot(mask):
    return jnp.where(mask, 1.0, 0.0).astype(BF16)


def iota(shape, dim):
    return lax.broadcasted_iota(jnp.int32, shape, dim)


def three_parts(x):
    first = x.astype(BF16)
    rest = x - first.astype(F32)
    second = rest.astype(BF16)
    third = (rest - second.astype(F32)).astype(BF16)
    return first, second, third


def kernel(
    embeds_hbm,
    ids_hbm,
    ranks_hbm,
    sizes_hbm,
    out,
    embeds,
    ids,
    ranks,
    sizes,
    unit,
    send,
    recv,
    sent_meta,
    column_meta,
    group_meta,
    place_of,
    look,
    gathered,
    blocks,
    tops,
    lows,
    shares,
    early,
    late,
    best,
    answers,
    returned,
    load_sem,
    again_sem,
    send_sem,
    recv_sem,
    column_send_sem,
    column_recv_sem,
    group_send_sem,
    group_recv_sem,
    block_send_sem,
    block_recv_sem,
    peer_send_sem,
    peer_recv_sem,
    forward_send_sem,
    forward_recv_sem,
    early_send_sem,
    early_recv_sem,
    late_send_sem,
    late_recv_sem,
    answer_send_sem,
    answer_recv_sem,
):
    rows, width = embeds.shape
    src = lax.axis_index("src")
    grp = lax.axis_index("grp")
    x, y = src >> 2, src & 3
    z, core = grp >> 1, grp & 1

    def src_at(n, sign):
        return ((x + sign * (n >> 2)) & 3) * 4 + ((y + sign * n) & 3)

    def grp_at(m, sign):
        return ((z + sign * (m >> 1)) & 3) * 2 + ((core + m) & 1)

    loads = []
    for n, (source, target) in enumerate(
        ((ids_hbm, ids), (ranks_hbm, ranks), (sizes_hbm, sizes), (embeds_hbm, embeds))
    ):
        copy = pltpu.make_async_copy(source, target, load_sem.at[n])
        copy.start()
        loads.append(copy)

    barrier = pltpu.get_barrier_semaphore()

    def greet_src(n, carry):
        pl.semaphore_signal(barrier, inc=1, device_id=(src_at(n, 1), grp), device_id_type=MESH)
        return carry

    def greet_grp(m, carry):
        pl.semaphore_signal(barrier, inc=1, device_id=(src, grp_at(m, 1)), device_id_type=MESH)
        return carry

    lax.fori_loop(1, SRC, greet_src, 0)
    lax.fori_loop(1, GRP, greet_grp, 0)

    for copy in loads[:3]:
        copy.wait()
    clusters = sizes.shape[1]
    size_row = sizes[...].astype(F32)
    earlier = iota((clusters, clusters), 1) < iota((clusters, clusters), 0)
    starts = jnp.sum(jnp.where(earlier, size_row, 0.0), axis=1, keepdims=True)
    mine = iota((clusters, rows), 0) == ids[...]
    start_row = jnp.sum(jnp.where(mine, starts, 0.0), axis=0, keepdims=True)
    position = start_row.astype(jnp.int32) + ranks[...]
    tiling = position >> 16
    to_x = (((position >> 15) & 1) * 2 + ((position >> 12) & 1) - tiling) & 3
    to_y = (((position >> 14) & 1) * 2 + ((position >> 11) & 1) - tiling) & 3
    to_z = (((position >> 13) & 1) * 2 + ((position >> 10) & 1) - tiling) & 3
    to_core = (position >> 9) & 1
    to_grp = to_z * 2 + to_core
    dx, dy, dz = (to_x - x) & 3, (to_y - y) & 3, (to_z - z) & 3
    dc = (to_core - core) & 1
    column_row = dx * 4 + dy
    step_row = ((column_row * GRP + dz * 2 + dc) * UNMIX) & (DEVICES - 1)
    to_step = one_hot(iota((DEVICES, rows), 0) == step_row)
    to_column = one_hot(iota((SRC, rows), 0) == column_row)

    part = 256
    before = one_hot(iota((part, part), 0) < iota((part, part), 1))
    carry = jnp.zeros((DEVICES, 1), F32)
    slot_parts = []
    for n in range(rows // part):
        piece = to_step[:, n * part : (n + 1) * part]
        piece32 = piece.astype(F32)
        count = dot(piece, before) + carry
        slot_parts.append(jnp.sum(piece32 * count, axis=0, keepdims=True))
        carry = carry + jnp.sum(piece32, axis=1, keepdims=True)
    slot_row = jnp.concatenate(slot_parts, axis=1).astype(jnp.int32)
    index_row = step_row * SLOTS + slot_row
    lane_hot = one_hot(iota((LANES, rows), 0) == to_grp * SLOTS + slot_row)

    place_row = tiling * HALF + (position & (HALF - 1)) + 1
    upper = to_column * (place_row >> 3).astype(F32).astype(BF16)
    lower = to_column * (place_row & 7).astype(F32).astype(BF16)
    meta = 8.0 * dot(upper, lane_hot, NT) + dot(lower, lane_hot, NT)
    for n in range(SRC):
        sent_meta[n] = meta[n : n + 1, :]
    column_meta[0] = sent_meta[0]

    pl.semaphore_wait(barrier, SRC - 1 + GRP - 1)

    def greet_again(m, carry):
        pl.semaphore_signal(again_sem, inc=1, device_id=(src, grp_at(m, 1)), device_id_type=MESH)
        return carry

    lax.fori_loop(1, GRP, greet_again, 0)

    def send_column_meta(n, carry):
        pltpu.make_async_remote_copy(
            src_ref=sent_meta.at[n],
            dst_ref=column_meta.at[n],
            send_sem=column_send_sem,
            recv_sem=column_recv_sem,
            device_id=(src_at(n, 1), grp),
            device_id_type=MESH,
        ).start()
        return carry

    lax.fori_loop(1, SRC, send_column_meta, 0)

    loads[3].wait()

    def normalise(n, carry):
        here = pl.ds(pl.multiple_of(n * part, part), part)
        wide = embeds[here, :].astype(F32)
        total = jnp.sum(wide * wide, axis=1, keepdims=True)
        unit[here, :] = (wide * lax.rsqrt(total + epsilon)).astype(BF16)
        return carry

    lax.fori_loop(0, rows // part, normalise, 0)

    def wait_all(ref, sem, count):
        pltpu.make_async_copy(ref.at[pl.ds(1, count)], ref.at[pl.ds(1, count)], sem).wait()

    for n in range(CLASSES):
        pick = one_hot(iota((CLASS_ROWS, rows), 0) + n * CLASS_ROWS == index_row)
        packed = dot(pick, unit[...]).astype(BF16)
        send[pl.ds(n * PER, PER)] = packed.reshape(PER, SLOTS, width)
        if n == 0:
            recv[0] = send[0]
            pl.semaphore_wait(again_sem, GRP - 1)

        def send_step(step, carry):
            k = (step * MIX) & (DEVICES - 1)
            pltpu.make_async_remote_copy(
                src_ref=send.at[step],
                dst_ref=recv.at[step],
                send_sem=send_sem.at[n],
                recv_sem=recv_sem.at[n],
                device_id=(src_at(k >> 3, 1), grp_at(k & 7, 1)),
                device_id_type=MESH,
            ).start()
            return carry

        lax.fori_loop(max(1, n * PER), (n + 1) * PER, send_step, 0)

        if n == 0:
            wait_all(column_meta, column_recv_sem, SRC - 1)
            group_meta[0] = column_meta[...]

            def send_group_meta(m, carry):
                pltpu.make_async_remote_copy(
                    src_ref=column_meta,
                    dst_ref=group_meta.at[m],
                    send_sem=group_send_sem,
                    recv_sem=group_recv_sem,
                    device_id=(src, grp_at(m, 1)),
                    device_id_type=MESH,
                ).start()
                return carry

            lax.fori_loop(1, GRP, send_group_meta, 0)

    lane_no = iota((1, LANES), 1)
    pick_rows = []
    for n in range(SRC):
        wanted = column_meta[n].astype(jnp.int32) - 1
        look[:, n * LANES : (n + 1) * LANES] = one_hot(iota((LANES, LANES), 0) == (wanted & 127))
        row_no = (lane_no // SLOTS) * 8 + (wanted >> 7)
        pick_rows.append(jnp.where(wanted >= 0, row_no, -1))
    pick_row = jnp.concatenate(pick_rows, axis=1)

    wait_all(group_meta, group_recv_sem, GRP - 1)

    all_meta = group_meta[...].reshape(DEVICES, LANES).astype(jnp.int32)
    choose = one_hot(iota((LANES, LANES), 0) == grp * SLOTS + (iota((LANES, LANES), 1) & 15))
    number = iota((DEVICES, LANES), 0)
    step_of = (((number & 15) * GRP + (number >> 4)) * UNMIX) & (DEVICES - 1)
    kept = (iota((DEVICES, LANES), 1) >> 4) == (step_of & 7)
    number = iota((SRC, DEVICES), 1)
    step_of = (((number & 15) * GRP + (number >> 4)) * UNMIX) & (DEVICES - 1)
    line_hot = one_hot((step_of >> 3) == iota((SRC, DEVICES), 0))
    got_places = jnp.zeros((SRC, LANES), F32)
    for scale, digit in ((8.0, all_meta >> 3), (1.0, all_meta & 7)):
        spread = dot(digit.astype(F32).astype(BF16), choose)
        spread = jnp.where(kept, spread, 0.0).astype(BF16)
        got_places += scale * dot(line_hot, spread)
    got_places = got_places.astype(jnp.int32)

    for n in range(CLASSES):
        for m in range(CLASS_ROWS // LANES):
            line = n * (CLASS_ROWS // LANES) + m
            hit = iota((rows, LANES), 0) + 1 == got_places[line : line + 1, :]
            place_of[n, :, m * LANES : (m + 1) * LANES] = one_hot(hit)

    def bits(tiling):
        return (x + tiling) & 1, (y + tiling) & 1, (z + tiling) & 1

    def across(tiling, *axes):
        place = [x, y, z]
        for axis in axes:
            place[axis] = (place[axis] + 1 - 2 * bits(tiling)[axis]) & 3
        return place

    def device_across(tiling, axes, to_core):
        to_x, to_y, to_z = across(tiling, *axes)
        return (to_x * 4 + to_y, to_z * 2 + to_core)

    def number(tiling, slot):
        v1, v2, v3 = bits(tiling)
        if not isinstance(slot, int) or slot < 2:
            own = slot
        elif slot == 2:
            v1, own = 1 - v1, core ^ v1
        elif slot == 3:
            v2, own = 1 - v2, core
        elif slot == 4:
            v3, own = 1 - v3, core ^ v2
        else:
            v2, v3, own = 1 - v2, 1 - v3, core
        return ((v1 * 2 + v2) * 2 + v3) * 2 + own

    def base(tiling):
        cube_x, cube_y, cube_z = (((i + tiling) & 3) >> 1 for i in (x, y, z))
        return (tiling * 8 + cube_x * 4 + cube_y * 2 + cube_z) * (GRP * rows)

    for tiling in range(2):
        for slot in range(HELD):
            places = number(tiling, slot) * HALF + base(tiling) + iota((1, HALF), 1)
            below = jnp.where(starts <= places.astype(F32), starts, 0.0)
            low = jnp.max(below, axis=0, keepdims=True)
            lows[tiling, slot] = low.astype(jnp.int32) - base(tiling)
            tops[tiling, slot] = jnp.full((1, HALF), -1.0, F32)

    def first_half(axis):
        return 1 if axis == 1 else 0

    def neighbour_copy(tiling, axis, half):
        v1, v2, v3 = bits(tiling)
        to_core = core ^ (1 - v1, 0, v2)[axis]
        here = pl.ds(half * QUARTER, QUARTER)
        return pltpu.make_async_remote_copy(
            src_ref=blocks.at[tiling, core, here],
            dst_ref=blocks.at[tiling, 2 + axis, here],
            send_sem=block_send_sem.at[tiling, axis, half],
            recv_sem=block_recv_sem.at[tiling, axis, half],
            device_id=device_across(tiling, (axis,), to_core),
            device_id_type=MESH,
        )

    def peer_copy(tiling):
        return pltpu.make_async_remote_copy(
            src_ref=blocks.at[tiling, core],
            dst_ref=blocks.at[tiling, core],
            send_sem=peer_send_sem.at[tiling],
            recv_sem=peer_recv_sem.at[tiling],
            device_id=(src, z * 2 + core ^ 1),
            device_id_type=MESH,
        )

    def forward_copy(tiling, axis):
        half = first_half(axis)
        here = pl.ds(half * QUARTER, QUARTER)
        to_core = core if axis == 1 else core ^ bits(tiling)[1]
        return pltpu.make_async_remote_copy(
            src_ref=blocks.at[tiling, 2 + axis, here],
            dst_ref=blocks.at[tiling, 5, here],
            send_sem=forward_send_sem.at[tiling, half],
            recv_sem=forward_recv_sem.at[tiling, half],
            device_id=device_across(tiling, (3 - axis,), to_core),
            device_id_type=MESH,
        )

    for n in range(CLASSES):
        first = 1 if n == 0 else 0
        group = recv.at[pl.ds(n * PER + first, PER - first)]
        pltpu.make_async_copy(group, group, recv_sem.at[n]).wait()
        arrived = recv[pl.ds(n * PER, PER)].reshape(CLASS_ROWS, width)
        for tiling in range(2):
            here = pl.ds(tiling * HALF, HALF)
            found = dot(place_of[n, here, :], arrived)
            if n == 0:
                gathered[here, :] = found
            elif n < CLASSES - 1:
                gathered[here, :] += found
            else:
                blocks[tiling, core] = (gathered[here, :] + found).astype(BF16)
                for axis in range(3):
                    neighbour_copy(tiling, axis, first_half(axis)).start()
                peer_copy(tiling).start()
                for axis in range(3):
                    neighbour_copy(tiling, axis, 1 - first_half(axis)).start()

    def score(tiling, key, query, same=False):
        key_slot, key_start, keys = key[:3]
        query_slot, query_start, queries = query[:3]
        products = dot(
            blocks[tiling, key_slot, pl.ds(key_start, keys), :],
            blocks[tiling, query_slot, pl.ds(query_start, queries), :],
            NT,
        )
        columns = slice(query_start, query_start + queries)
        key_no = iota((keys, queries), 0) + key_start
        allowed = key_no >= lows[tiling, query_slot][:, columns] - key[3] * HALF
        if same:
            allowed = allowed & (key_no < iota((keys, queries), 1) + query_start)
        found = jnp.max(jnp.where(allowed, products, -1.0), axis=0, keepdims=True)
        tops[tiling, query_slot, :, columns] = jnp.maximum(
            tops[tiling, query_slot, :, columns], found
        )

    def pair(tiling, a, b):
        a, b = (*a, number(tiling, a[0])), (*b, number(tiling, b[0]))
        a_first = a[3] < b[3]

        @pl.when(a_first)
        def _():
            score(tiling, a, b)

        @pl.when(jnp.logical_not(a_first))
        def _():
            score(tiling, b, a)

    def own_slot(tiling, axis):
        v1, v2, v3 = bits(tiling)
        return core ^ (0, v2, v2 ^ v3)[axis]

    def own_scores(tiling, carry):
        mine = (core, 0, HALF, number(tiling, core))
        score(tiling, mine, mine, True)
        peer = blocks.at[tiling, core ^ 1]
        pltpu.make_async_copy(peer, peer, peer_recv_sem.at[tiling]).wait()
        start = pl.multiple_of(core * QUARTER, QUARTER)
        key = (0, start, QUARTER, number(tiling, 0))
        score(tiling, key, (1, 0, HALF, number(tiling, 1)))
        return carry

    lax.fori_loop(0, 2, own_scores, 0)

    def wait_neighbour(tiling, axis, half):
        here = blocks.at[tiling, 2 + axis, pl.ds(half * QUARTER, QUARTER)]
        pltpu.make_async_copy(here, here, block_recv_sem.at[tiling, axis, half]).wait()

    def forward(tiling, carry):
        for axis in (1, 2):
            wait_neighbour(tiling, axis, first_half(axis))
            forward_copy(tiling, axis).start()
        return carry

    lax.fori_loop(0, 2, forward, 0)

    def held_part(axis, half):
        return (2 + axis, half * QUARTER, QUARTER)

    def first_scores(tiling, carry):
        wait_neighbour(tiling, 0, first_half(0))
        for axis in range(3):
            own = (own_slot(tiling, axis), 0, HALF)
            pair(tiling, own, held_part(axis, first_half(axis)))
        for axis, other in ((0, 1), (0, 2), (1, 2)):
            pair(
                tiling, held_part(axis, first_half(axis)), held_part(other, first_half(other))
            )
        return carry

    lax.fori_loop(0, 2, first_scores, 0)

    def second_scores(tiling, carry):
        for axis in range(3):
            wait_neighbour(tiling, axis, 1 - first_half(axis))
            own = (own_slot(tiling, axis), 0, HALF)
            pair(tiling, own, held_part(axis, 1 - first_half(axis)))
        for axis, other in ((0, 1), (0, 2), (1, 2)):
            pair(tiling, held_part(axis, 1 - first_half(axis)), (2 + other, 0, HALF))
            pair(
                tiling,
                held_part(axis, first_half(axis)),
                held_part(other, 1 - first_half(other)),
            )
        return carry

    lax.fori_loop(0, 2, second_scores, 0)

    def stage(kind, slot, tiling):
        for n in range(HALF // LANES):
            line = tops[tiling, slot, :, n * LANES : (n + 1) * LANES]
            shares[tiling * 6 + kind, n : n + 1, :] = line

    def send_found(kind, tiling, target, owner, to_all, send_sem, recv_sem):
        source = shares.at[tiling * 6 + kind]
        if kind < 4:
            place = early.at[owner * 8 + tiling * 4 + kind]
        else:
            place = late.at[owner * 4 + tiling * 2 + kind - 4]

        def send_one(m, carry):
            pltpu.make_async_remote_copy(
                src_ref=source,
                dst_ref=place,
                send_sem=send_sem,
                recv_sem=recv_sem,
                device_id=(target, grp_at(m, 1)),
                device_id_type=MESH,
            ).start()
            return carry

        lax.fori_loop(0 if to_all else 1, GRP, send_one, 0)
        if not to_all:
            place[...] = source[...]

    for tiling in range(2):
        v2 = bits(tiling)[1]
        for kind, slot in enumerate((core, core ^ 1, 3, 4)):
            stage(kind, slot, tiling)
        send_found(0, tiling, src, grp, False, early_send_sem, early_recv_sem)
        send_found(1, tiling, src, grp ^ 1, False, early_send_sem, early_recv_sem)
        target, owner = device_across(tiling, (1,), core)
        send_found(2, tiling, target, owner, True, early_send_sem, early_recv_sem)
        target, owner = device_across(tiling, (2,), core ^ v2)
        send_found(3, tiling, src, owner, False, early_send_sem, early_recv_sem)

    def far_scores(tiling, carry):
        for half in range(2):
            here = blocks.at[tiling, 5, pl.ds(half * QUARTER, QUARTER)]
            pltpu.make_async_copy(here, here, forward_recv_sem.at[tiling, half]).wait()
            pair(tiling, (2, 0, HALF), (5, half * QUARTER, QUARTER))
        return carry

    lax.fori_loop(0, 2, far_scores, 0)

    for tiling in range(2):
        v1 = bits(tiling)[0]
        stage(4, 2, tiling)
        stage(5, 5, tiling)
        target, owner = device_across(tiling, (0,), core ^ v1)
        send_found(4, tiling, target, owner, True, late_send_sem, late_recv_sem)
        target, owner = device_across(tiling, (1, 2), core)
        send_found(5, tiling, target, owner, True, late_send_sem, late_recv_sem)

    def wait_early(sem):
        here = early.at[pl.ds(0, EARLY)]
        pltpu.make_async_copy(here, here, sem).wait()

    wait_early(early_recv_sem)
    for owner in range(GRP):
        for tiling in range(2):
            line = owner * 8 + tiling * 4
            early[line] = jnp.maximum(
                jnp.maximum(early[line], early[line + 1]),
                jnp.maximum(early[line + 2], early[line + 3]),
            )
    pltpu.make_async_copy(late, late, late_recv_sem).wait()
    for owner in range(GRP):
        added = []
        for tiling in range(2):
            line = owner * 4 + tiling * 2
            last = jnp.maximum(late[line], late[line + 1])
            added.append(jnp.maximum(early[owner * 8 + tiling * 4], last))
        best[owner] = jnp.concatenate(added, axis=0)

    answer = jnp.zeros((GRP * rows // LANES, SRC * LANES), F32)
    for piece in three_parts(best[...].reshape(GRP * rows // LANES, LANES)):
        answer += dot(piece, look[...])
    right = iota(answer.shape, 0) == pick_row
    answer = jnp.sum(jnp.where(right, answer, 0.0), axis=0, keepdims=True)
    for n in range(SRC):
        answers[n] = answer[:, n * LANES : (n + 1) * LANES]
    returned[0] = answers[0]

    def send_answer(n, carry):
        pltpu.make_async_remote_copy(
            src_ref=answers.at[n],
            dst_ref=returned.at[n],
            send_sem=answer_send_sem,
            recv_sem=answer_recv_sem,
            device_id=(src_at(n, -1), grp),
            device_id_type=MESH,
        ).start()
        return carry

    lax.fori_loop(1, SRC, send_answer, 0)
    wait_all(returned, answer_recv_sem, SRC - 1)
    table = returned[...].reshape(SRC, LANES).T
    chosen = jnp.zeros((LANES, rows), F32)
    for piece in three_parts(table):
        chosen += dot(piece, to_column)
    out[...] = jnp.sum(chosen * lane_hot.astype(F32), axis=0, keepdims=True)

    wait_all(sent_meta, column_send_sem, SRC - 1)
    wait_all(group_meta, group_send_sem, GRP - 1)
    wait_early(early_send_sem)
    pltpu.make_async_copy(late, late, late_send_sem).wait()
    wait_all(answers, answer_send_sem, SRC - 1)
    for n in range(CLASSES):
        first = 1 if n == 0 else 0
        group = send.at[pl.ds(n * PER + first, PER - first)]
        pltpu.make_async_copy(group, group, send_sem.at[n]).wait()
    for tiling in range(2):
        whole = blocks.at[tiling, core]
        pltpu.make_async_copy(whole, whole, peer_send_sem.at[tiling]).wait()
        for half in range(2):
            here = blocks.at[tiling, core, pl.ds(half * QUARTER, QUARTER)]
            for axis in range(3):
                pltpu.make_async_copy(here, here, block_send_sem.at[tiling, axis, half]).wait()
            pltpu.make_async_copy(here, here, forward_send_sem.at[tiling, half]).wait()


def on_device(embeds, cluster_id, cluster_rank, cluster_size):
    rows, width = embeds.shape
    clusters = cluster_size.shape[0]
    best = pl.pallas_call(
        kernel,
        out_shape=jax.ShapeDtypeStruct((1, rows), F32),
        in_specs=[pl.BlockSpec(memory_space=pl.ANY)] * 4,
        out_specs=pl.BlockSpec(memory_space=pltpu.VMEM),
        scratch_shapes=[
            pltpu.VMEM((rows, width), BF16),
            pltpu.VMEM((1, rows), jnp.int32),
            pltpu.VMEM((1, rows), jnp.int32),
            pltpu.VMEM((1, clusters), jnp.int32),
            pltpu.VMEM((rows, width), BF16),
            pltpu.VMEM((DEVICES, SLOTS, width), BF16),
            pltpu.VMEM((DEVICES, SLOTS, width), BF16),
            pltpu.VMEM((SRC, 1, LANES), F32),
            pltpu.VMEM((SRC, 1, LANES), F32),
            pltpu.VMEM((GRP, SRC, 1, LANES), F32),
            pltpu.VMEM((CLASSES, rows, CLASS_ROWS), BF16),
            pltpu.VMEM((LANES, SRC * LANES), BF16),
            pltpu.VMEM((rows, width), F32),
            pltpu.VMEM((2, HELD, HALF, width), BF16),
            pltpu.VMEM((2, HELD, 1, HALF), F32),
            pltpu.VMEM((2, HELD, 1, HALF), jnp.int32),
            pltpu.VMEM((12, HALF // LANES, LANES), F32),
            pltpu.VMEM((GRP * 8, HALF // LANES, LANES), F32),
            pltpu.VMEM((GRP * 4, HALF // LANES, LANES), F32),
            pltpu.VMEM((GRP, rows // LANES, LANES), F32),
            pltpu.VMEM((SRC, 1, LANES), F32),
            pltpu.VMEM((SRC, 1, LANES), F32),
            pltpu.SemaphoreType.DMA((4,)),
            pltpu.SemaphoreType.REGULAR,
            pltpu.SemaphoreType.DMA((CLASSES,)),
            pltpu.SemaphoreType.DMA((CLASSES,)),
            pltpu.SemaphoreType.DMA,
            pltpu.SemaphoreType.DMA,
            pltpu.SemaphoreType.DMA,
            pltpu.SemaphoreType.DMA,
            pltpu.SemaphoreType.DMA((2, 3, 2)),
            pltpu.SemaphoreType.DMA((2, 3, 2)),
            pltpu.SemaphoreType.DMA((2,)),
            pltpu.SemaphoreType.DMA((2,)),
            pltpu.SemaphoreType.DMA((2, 2)),
            pltpu.SemaphoreType.DMA((2, 2)),
            pltpu.SemaphoreType.DMA,
            pltpu.SemaphoreType.DMA,
            pltpu.SemaphoreType.DMA,
            pltpu.SemaphoreType.DMA,
            pltpu.SemaphoreType.DMA,
            pltpu.SemaphoreType.DMA,
        ],
        compiler_params=pltpu.CompilerParams(
            collective_id=0, has_side_effects=True, vmem_limit_bytes=50 * 1024 * 1024
        ),
        name="dedup",
    )(
        embeds,
        cluster_id.reshape(1, rows),
        cluster_rank.reshape(1, rows),
        cluster_size.reshape(1, -1),
    )
    return best.reshape(rows)


def solution(mesh):
    placed = (P(("src", "grp"), None), P(("src", "grp")), P(("src", "grp")), P())
    return jax.shard_map(
        on_device, mesh=mesh, in_specs=placed, out_specs=P(("src", "grp")), check_vma=False
    )
```

```python
import jax
import jax.numpy as jnp
from jax import lax
from jax.experimental import pallas as pl
from jax.experimental.pallas import tpu as pltpu
from jax.sharding import PartitionSpec as P

MESH = pl.DeviceIdType.MESH
F32 = jnp.float32
BF16 = jnp.bfloat16

epsilon = 1e-06

DEVICES = 128
SRC = 16
GRP = 8
LANES = 128
SLOTS = 16
CLASSES = 4
PER = DEVICES // CLASSES
CLASS_ROWS = PER * SLOTS
HALF = 512
QUARTER = 256
HELD = 6
EARLY = 66
MIX, UNMIX = 53, 29

NN = (((1,), (0,)), ((), ()))
NT = (((1,), (1,)), ((), ()))


def dot(a, b, dims=NN):
    return lax.dot_general(a, b, dims, preferred_element_type=F32)


def one_hot(mask):
    return jnp.where(mask, 1.0, 0.0).astype(BF16)


def iota(shape, dim):
    return lax.broadcasted_iota(jnp.int32, shape, dim)


def three_parts(x):
    first = x.astype(BF16)
    rest = x - first.astype(F32)
    second = rest.astype(BF16)
    third = (rest - second.astype(F32)).astype(BF16)
    return first, second, third


def kernel(
    embeds_hbm,
    ids_hbm,
    ranks_hbm,
    sizes_hbm,
    out,
    embeds,
    ids,
    ranks,
    sizes,
    unit,
    send,
    recv,
    sent_meta,
    column_meta,
    group_meta,
    place_of,
    look,
    gathered,
    blocks,
    tops,
    lows,
    shares,
    early,
    late,
    best,
    answers,
    returned,
    load_sem,
    again_sem,
    send_sem,
    recv_sem,
    column_send_sem,
    column_recv_sem,
    group_send_sem,
    group_recv_sem,
    block_send_sem,
    block_recv_sem,
    peer_send_sem,
    peer_recv_sem,
    forward_send_sem,
    forward_recv_sem,
    early_send_sem,
    early_recv_sem,
    late_send_sem,
    late_recv_sem,
    answer_send_sem,
    answer_recv_sem,
):
    rows, width = embeds.shape
    src = lax.axis_index("src")
    grp = lax.axis_index("grp")
    x, y = src >> 2, src & 3
    z, core = grp >> 1, grp & 1

    def src_at(n, sign):
        return ((x + sign * (n >> 2)) & 3) * 4 + ((y + sign * n) & 3)

    def grp_at(m, sign):
        return ((z + sign * (m >> 1)) & 3) * 2 + ((core + m) & 1)

    barrier = pltpu.get_barrier_semaphore()

    def greet_src(n, carry):
        pl.semaphore_signal(barrier, inc=1, device_id=(src_at(n, 1), grp), device_id_type=MESH)
        return carry

    def greet_grp(m, carry):
        pl.semaphore_signal(barrier, inc=1, device_id=(src, grp_at(m, 1)), device_id_type=MESH)
        return carry

    lax.fori_loop(1, SRC, greet_src, 0)
    lax.fori_loop(1, GRP, greet_grp, 0)

    loads = []
    for n, (source, target) in enumerate(
        ((ids_hbm, ids), (ranks_hbm, ranks), (sizes_hbm, sizes), (embeds_hbm, embeds))
    ):
        copy = pltpu.make_async_copy(source, target, load_sem.at[n])
        copy.start()
        loads.append(copy)

    for copy in loads[:3]:
        copy.wait()
    clusters = sizes.shape[1]
    size_row = sizes[...].astype(F32)
    earlier = iota((clusters, clusters), 1) < iota((clusters, clusters), 0)
    starts = jnp.sum(jnp.where(earlier, size_row, 0.0), axis=1, keepdims=True)
    mine = iota((clusters, rows), 0) == ids[...]
    start_row = jnp.sum(jnp.where(mine, starts, 0.0), axis=0, keepdims=True)
    position = start_row.astype(jnp.int32) + ranks[...]
    tiling = position >> 16
    to_x = (((position >> 15) & 1) * 2 + ((position >> 12) & 1) - tiling) & 3
    to_y = (((position >> 14) & 1) * 2 + ((position >> 11) & 1) - tiling) & 3
    to_z = (((position >> 13) & 1) * 2 + ((position >> 10) & 1) - tiling) & 3
    to_core = (position >> 9) & 1
    to_grp = to_z * 2 + to_core
    dx, dy, dz = (to_x - x) & 3, (to_y - y) & 3, (to_z - z) & 3
    dc = (to_core - core) & 1
    column_row = dx * 4 + dy
    step_row = ((column_row * GRP + dz * 2 + dc) * UNMIX) & (DEVICES - 1)
    to_step = one_hot(iota((DEVICES, rows), 0) == step_row)
    to_column = one_hot(iota((SRC, rows), 0) == column_row)

    part = 256
    before = one_hot(iota((part, part), 0) < iota((part, part), 1))
    carry = jnp.zeros((DEVICES, 1), F32)
    slot_parts = []
    for n in range(rows // part):
        piece = to_step[:, n * part : (n + 1) * part]
        piece32 = piece.astype(F32)
        count = dot(piece, before) + carry
        slot_parts.append(jnp.sum(piece32 * count, axis=0, keepdims=True))
        carry = carry + jnp.sum(piece32, axis=1, keepdims=True)
    slot_row = jnp.concatenate(slot_parts, axis=1).astype(jnp.int32)
    index_row = step_row * SLOTS + slot_row
    lane_hot = one_hot(iota((LANES, rows), 0) == to_grp * SLOTS + slot_row)

    place_row = tiling * HALF + (position & (HALF - 1)) + 1
    upper = to_column * (place_row >> 3).astype(F32).astype(BF16)
    lower = to_column * (place_row & 7).astype(F32).astype(BF16)
    meta = 8.0 * dot(upper, lane_hot, NT) + dot(lower, lane_hot, NT)
    for n in range(SRC):
        sent_meta[n] = meta[n : n + 1, :]
    column_meta[0] = sent_meta[0]

    pl.semaphore_wait(barrier, SRC - 1 + GRP - 1)

    def greet_again(m, carry):
        pl.semaphore_signal(again_sem, inc=1, device_id=(src, grp_at(m, 1)), device_id_type=MESH)
        return carry

    lax.fori_loop(1, GRP, greet_again, 0)

    def send_column_meta(n, carry):
        pltpu.make_async_remote_copy(
            src_ref=sent_meta.at[n],
            dst_ref=column_meta.at[n],
            send_sem=column_send_sem,
            recv_sem=column_recv_sem,
            device_id=(src_at(n, 1), grp),
            device_id_type=MESH,
        ).start()
        return carry

    lax.fori_loop(1, SRC, send_column_meta, 0)

    loads[3].wait()

    def normalise(n, carry):
        here = pl.ds(pl.multiple_of(n * part, part), part)
        wide = embeds[here, :].astype(F32)
        total = jnp.sum(wide * wide, axis=1, keepdims=True)
        unit[here, :] = (wide * lax.rsqrt(total + epsilon)).astype(BF16)
        return carry

    lax.fori_loop(0, rows // part, normalise, 0)

    def wait_all(ref, sem, count):
        pltpu.make_async_copy(ref.at[pl.ds(1, count)], ref.at[pl.ds(1, count)], sem).wait()

    for n in range(CLASSES):
        pick = one_hot(iota((CLASS_ROWS, rows), 0) + n * CLASS_ROWS == index_row)
        packed = dot(pick, unit[...]).astype(BF16)
        send[pl.ds(n * PER, PER)] = packed.reshape(PER, SLOTS, width)
        if n == 0:
            recv[0] = send[0]
            pl.semaphore_wait(again_sem, GRP - 1)

        def send_step(step, carry):
            k = (step * MIX) & (DEVICES - 1)
            pltpu.make_async_remote_copy(
                src_ref=send.at[step],
                dst_ref=recv.at[step],
                send_sem=send_sem.at[n],
                recv_sem=recv_sem.at[n],
                device_id=(src_at(k >> 3, 1), grp_at(k & 7, 1)),
                device_id_type=MESH,
            ).start()
            return carry

        lax.fori_loop(max(1, n * PER), (n + 1) * PER, send_step, 0)

        if n == 0:
            wait_all(column_meta, column_recv_sem, SRC - 1)
            group_meta[0] = column_meta[...]

            def send_group_meta(m, carry):
                pltpu.make_async_remote_copy(
                    src_ref=column_meta,
                    dst_ref=group_meta.at[m],
                    send_sem=group_send_sem,
                    recv_sem=group_recv_sem,
                    device_id=(src, grp_at(m, 1)),
                    device_id_type=MESH,
                ).start()
                return carry

            lax.fori_loop(1, GRP, send_group_meta, 0)

    lane_no = iota((1, LANES), 1)
    pick_rows = []
    for n in range(SRC):
        wanted = column_meta[n].astype(jnp.int32) - 1
        look[:, n * LANES : (n + 1) * LANES] = one_hot(iota((LANES, LANES), 0) == (wanted & 127))
        row_no = (lane_no // SLOTS) * 8 + (wanted >> 7)
        pick_rows.append(jnp.where(wanted >= 0, row_no, -1))
    pick_row = jnp.concatenate(pick_rows, axis=1)

    wait_all(group_meta, group_recv_sem, GRP - 1)

    all_meta = group_meta[...].reshape(DEVICES, LANES).astype(jnp.int32)
    choose = one_hot(iota((LANES, LANES), 0) == grp * SLOTS + (iota((LANES, LANES), 1) & 15))
    number = iota((DEVICES, LANES), 0)
    step_of = (((number & 15) * GRP + (number >> 4)) * UNMIX) & (DEVICES - 1)
    kept = (iota((DEVICES, LANES), 1) >> 4) == (step_of & 7)
    number = iota((SRC, DEVICES), 1)
    step_of = (((number & 15) * GRP + (number >> 4)) * UNMIX) & (DEVICES - 1)
    line_hot = one_hot((step_of >> 3) == iota((SRC, DEVICES), 0))
    got_places = jnp.zeros((SRC, LANES), F32)
    for scale, digit in ((8.0, all_meta >> 3), (1.0, all_meta & 7)):
        spread = dot(digit.astype(F32).astype(BF16), choose)
        spread = jnp.where(kept, spread, 0.0).astype(BF16)
        got_places += scale * dot(line_hot, spread)
    got_places = got_places.astype(jnp.int32)

    for n in range(CLASSES):
        for m in range(CLASS_ROWS // LANES):
            line = n * (CLASS_ROWS // LANES) + m
            hit = iota((rows, LANES), 0) + 1 == got_places[line : line + 1, :]
            place_of[n, :, m * LANES : (m + 1) * LANES] = one_hot(hit)

    def bits(tiling):
        return (x + tiling) & 1, (y + tiling) & 1, (z + tiling) & 1

    def across(tiling, *axes):
        place = [x, y, z]
        for axis in axes:
            place[axis] = (place[axis] + 1 - 2 * bits(tiling)[axis]) & 3
        return place

    def device_across(tiling, axes, to_core):
        to_x, to_y, to_z = across(tiling, *axes)
        return (to_x * 4 + to_y, to_z * 2 + to_core)

    def number(tiling, slot):
        v1, v2, v3 = bits(tiling)
        if not isinstance(slot, int) or slot < 2:
            own = slot
        elif slot == 2:
            v1, own = 1 - v1, core ^ v1
        elif slot == 3:
            v2, own = 1 - v2, core
        elif slot == 4:
            v3, own = 1 - v3, core ^ v2
        else:
            v2, v3, own = 1 - v2, 1 - v3, core
        return ((v1 * 2 + v2) * 2 + v3) * 2 + own

    def base(tiling):
        cube_x, cube_y, cube_z = (((i + tiling) & 3) >> 1 for i in (x, y, z))
        return (tiling * 8 + cube_x * 4 + cube_y * 2 + cube_z) * (GRP * rows)

    for tiling in range(2):
        for slot in range(HELD):
            places = number(tiling, slot) * HALF + base(tiling) + iota((1, HALF), 1)
            below = jnp.where(starts <= places.astype(F32), starts, 0.0)
            low = jnp.max(below, axis=0, keepdims=True)
            lows[tiling, slot] = low.astype(jnp.int32) - base(tiling)
            tops[tiling, slot] = jnp.full((1, HALF), -1.0, F32)

    def first_half(axis):
        return 1 if axis == 1 else 0

    def neighbour_copy(tiling, axis, half):
        v1, v2, v3 = bits(tiling)
        to_core = core ^ (1 - v1, 0, v2)[axis]
        here = pl.ds(half * QUARTER, QUARTER)
        return pltpu.make_async_remote_copy(
            src_ref=blocks.at[tiling, core, here],
            dst_ref=blocks.at[tiling, 2 + axis, here],
            send_sem=block_send_sem.at[tiling, axis, half],
            recv_sem=block_recv_sem.at[tiling, axis, half],
            device_id=device_across(tiling, (axis,), to_core),
            device_id_type=MESH,
        )

    def peer_copy(tiling):
        return pltpu.make_async_remote_copy(
            src_ref=blocks.at[tiling, core],
            dst_ref=blocks.at[tiling, core],
            send_sem=peer_send_sem.at[tiling],
            recv_sem=peer_recv_sem.at[tiling],
            device_id=(src, z * 2 + core ^ 1),
            device_id_type=MESH,
        )

    def forward_copy(tiling, axis):
        half = first_half(axis)
        here = pl.ds(half * QUARTER, QUARTER)
        to_core = core if axis == 1 else core ^ bits(tiling)[1]
        return pltpu.make_async_remote_copy(
            src_ref=blocks.at[tiling, 2 + axis, here],
            dst_ref=blocks.at[tiling, 5, here],
            send_sem=forward_send_sem.at[tiling, half],
            recv_sem=forward_recv_sem.at[tiling, half],
            device_id=device_across(tiling, (3 - axis,), to_core),
            device_id_type=MESH,
        )

    for n in range(CLASSES):
        first = 1 if n == 0 else 0
        group = recv.at[pl.ds(n * PER + first, PER - first)]
        pltpu.make_async_copy(group, group, recv_sem.at[n]).wait()
        arrived = recv[pl.ds(n * PER, PER)].reshape(CLASS_ROWS, width)
        for tiling in range(2):
            here = pl.ds(tiling * HALF, HALF)
            found = dot(place_of[n, here, :], arrived)
            if n == 0:
                gathered[here, :] = found
            elif n < CLASSES - 1:
                gathered[here, :] += found
            else:
                blocks[tiling, core] = (gathered[here, :] + found).astype(BF16)
                for axis in range(3):
                    neighbour_copy(tiling, axis, first_half(axis)).start()
                peer_copy(tiling).start()
                for axis in range(3):
                    neighbour_copy(tiling, axis, 1 - first_half(axis)).start()

    def score(tiling, key, query, same=False):
        key_slot, key_start, keys = key[:3]
        query_slot, query_start, queries = query[:3]
        products = dot(
            blocks[tiling, key_slot, pl.ds(key_start, keys), :],
            blocks[tiling, query_slot, pl.ds(query_start, queries), :],
            NT,
        )
        columns = slice(query_start, query_start + queries)
        key_no = iota((keys, queries), 0) + key_start
        allowed = key_no >= lows[tiling, query_slot][:, columns] - key[3] * HALF
        if same:
            allowed = allowed & (key_no < iota((keys, queries), 1) + query_start)
        found = jnp.max(jnp.where(allowed, products, -1.0), axis=0, keepdims=True)
        tops[tiling, query_slot, :, columns] = jnp.maximum(
            tops[tiling, query_slot, :, columns], found
        )

    def pair(tiling, a, b):
        a, b = (*a, number(tiling, a[0])), (*b, number(tiling, b[0]))
        a_first = a[3] < b[3]

        @pl.when(a_first)
        def _():
            score(tiling, a, b)

        @pl.when(jnp.logical_not(a_first))
        def _():
            score(tiling, b, a)

    def own_slot(tiling, axis):
        v1, v2, v3 = bits(tiling)
        return core ^ (0, v2, v2 ^ v3)[axis]

    def own_scores(tiling, carry):
        mine = (core, 0, HALF, number(tiling, core))
        score(tiling, mine, mine, True)
        peer = blocks.at[tiling, core ^ 1]
        pltpu.make_async_copy(peer, peer, peer_recv_sem.at[tiling]).wait()
        start = pl.multiple_of(core * QUARTER, QUARTER)
        key = (0, start, QUARTER, number(tiling, 0))
        score(tiling, key, (1, 0, HALF, number(tiling, 1)))
        return carry

    lax.fori_loop(0, 2, own_scores, 0)

    def wait_neighbour(tiling, axis, half):
        here = blocks.at[tiling, 2 + axis, pl.ds(half * QUARTER, QUARTER)]
        pltpu.make_async_copy(here, here, block_recv_sem.at[tiling, axis, half]).wait()

    def forward(tiling, carry):
        for axis in (1, 2):
            wait_neighbour(tiling, axis, first_half(axis))
            forward_copy(tiling, axis).start()
        return carry

    lax.fori_loop(0, 2, forward, 0)

    def held_part(axis, half):
        return (2 + axis, half * QUARTER, QUARTER)

    def first_scores(tiling, carry):
        wait_neighbour(tiling, 0, first_half(0))
        for axis in range(3):
            own = (own_slot(tiling, axis), 0, HALF)
            pair(tiling, own, held_part(axis, first_half(axis)))
        for axis, other in ((0, 1), (0, 2), (1, 2)):
            pair(
                tiling, held_part(axis, first_half(axis)), held_part(other, first_half(other))
            )
        return carry

    lax.fori_loop(0, 2, first_scores, 0)

    def second_scores(tiling, carry):
        for axis in range(3):
            wait_neighbour(tiling, axis, 1 - first_half(axis))
            own = (own_slot(tiling, axis), 0, HALF)
            pair(tiling, own, held_part(axis, 1 - first_half(axis)))
        for axis, other in ((0, 1), (0, 2), (1, 2)):
            pair(tiling, held_part(axis, 1 - first_half(axis)), (2 + other, 0, HALF))
            pair(
                tiling,
                held_part(axis, first_half(axis)),
                held_part(other, 1 - first_half(other)),
            )
        return carry

    lax.fori_loop(0, 2, second_scores, 0)

    zero_tiling = x & 1
    one_tiling = 1 - zero_tiling

    def stage(line, slot, tiling):
        for n in range(HALF // LANES):
            shares[line, n : n + 1, :] = tops[tiling, slot, :, n * LANES : (n + 1) * LANES]

    def send_found(line, target, owner, to_all, send_sem, recv_sem):
        source = shares.at[line]
        if line < 9:
            place = early.at[owner * 9 + line]
        else:
            place = late.at[owner * 2 + line - 9]

        def send_one(m, carry):
            pltpu.make_async_remote_copy(
                src_ref=source,
                dst_ref=place,
                send_sem=send_sem,
                recv_sem=recv_sem,
                device_id=(target, grp_at(m, 1)),
                device_id_type=MESH,
            ).start()
            return carry

        lax.fori_loop(0 if to_all else 1, GRP, send_one, 0)
        if not to_all:
            place[...] = source[...]

    for tiling in range(2):
        v2 = bits(tiling)[1]
        for kind, slot in enumerate((core, core ^ 1, 3, 4)):
            stage(tiling * 4 + kind, slot, tiling)
        line = tiling * 4
        send_found(line, src, grp, False, early_send_sem, early_recv_sem)
        send_found(line + 1, src, grp ^ 1, False, early_send_sem, early_recv_sem)
        target, owner = device_across(tiling, (1,), core)
        send_found(line + 2, target, owner, True, early_send_sem, early_recv_sem)
        target, owner = device_across(tiling, (2,), core ^ v2)
        send_found(line + 3, src, owner, False, early_send_sem, early_recv_sem)
    stage(8, 2, one_tiling)
    target, owner = device_across(one_tiling, (0,), core ^ 1)
    send_found(8, target, owner, True, early_send_sem, early_recv_sem)

    def far_scores(tiling, carry):
        for half in range(2):
            here = blocks.at[tiling, 5, pl.ds(half * QUARTER, QUARTER)]
            pltpu.make_async_copy(here, here, forward_recv_sem.at[tiling, half]).wait()
            pair(tiling, (2, 0, HALF), (5, half * QUARTER, QUARTER))
        return carry

    lax.fori_loop(0, 2, far_scores, 0)

    stage(9, 2, zero_tiling)
    target, owner = device_across(zero_tiling, (0,), core)
    send_found(9, target, owner, True, late_send_sem, late_recv_sem)
    stage(10, 5, one_tiling)
    target, owner = device_across(one_tiling, (1, 2), core)
    send_found(10, target, owner, True, late_send_sem, late_recv_sem)

    def wait_early(sem):
        here = early.at[pl.ds(0, EARLY)]
        pltpu.make_async_copy(here, here, sem).wait()

    wait_early(early_recv_sem)
    for owner in range(GRP):
        for tiling in range(2):
            line = owner * 9 + tiling * 4
            early[line] = jnp.maximum(
                jnp.maximum(early[line], early[line + 1]),
                jnp.maximum(early[line + 2], early[line + 3]),
            )
    pltpu.make_async_copy(late, late, late_recv_sem).wait()
    for owner in range(GRP):
        line = owner * 9
        to_zero, to_one = early[line + 8], jnp.maximum(late[owner * 2], late[owner * 2 + 1])
        added = (
            jnp.maximum(early[line], jnp.where(zero_tiling == 0, to_zero, to_one)),
            jnp.maximum(early[line + 4], jnp.where(zero_tiling == 0, to_one, to_zero)),
        )
        best[owner] = jnp.concatenate(added, axis=0)

    lines = GRP * rows // LANES
    parts = jnp.concatenate(three_parts(best[...].reshape(lines, LANES)), axis=0)
    answer = dot(parts, look[...])
    answer = answer[:lines] + answer[lines : 2 * lines] + answer[2 * lines :]
    right = iota(answer.shape, 0) == pick_row
    answer = jnp.sum(jnp.where(right, answer, 0.0), axis=0, keepdims=True)
    for n in range(SRC):
        answers[n] = answer[:, n * LANES : (n + 1) * LANES]
    returned[0] = answers[0]

    def send_answer(n, carry):
        pltpu.make_async_remote_copy(
            src_ref=answers.at[n],
            dst_ref=returned.at[n],
            send_sem=answer_send_sem,
            recv_sem=answer_recv_sem,
            device_id=(src_at(n, -1), grp),
            device_id_type=MESH,
        ).start()
        return carry

    lax.fori_loop(1, SRC, send_answer, 0)
    wait_all(returned, answer_recv_sem, SRC - 1)
    table = returned[...].reshape(SRC, LANES).T
    parts = jnp.concatenate(three_parts(table), axis=1)
    chosen = dot(parts, jnp.concatenate([to_column] * 3, axis=0))
    out[...] = jnp.sum(chosen * lane_hot.astype(F32), axis=0, keepdims=True)

    wait_all(sent_meta, column_send_sem, SRC - 1)
    wait_all(group_meta, group_send_sem, GRP - 1)
    wait_early(early_send_sem)
    pltpu.make_async_copy(late, late, late_send_sem).wait()
    wait_all(answers, answer_send_sem, SRC - 1)
    for n in range(CLASSES):
        first = 1 if n == 0 else 0
        group = send.at[pl.ds(n * PER + first, PER - first)]
        pltpu.make_async_copy(group, group, send_sem.at[n]).wait()
    for tiling in range(2):
        whole = blocks.at[tiling, core]
        pltpu.make_async_copy(whole, whole, peer_send_sem.at[tiling]).wait()
        for half in range(2):
            here = blocks.at[tiling, core, pl.ds(half * QUARTER, QUARTER)]
            for axis in range(3):
                pltpu.make_async_copy(here, here, block_send_sem.at[tiling, axis, half]).wait()
            pltpu.make_async_copy(here, here, forward_send_sem.at[tiling, half]).wait()


def on_device(embeds, cluster_id, cluster_rank, cluster_size):
    rows, width = embeds.shape
    clusters = cluster_size.shape[0]
    best = pl.pallas_call(
        kernel,
        out_shape=jax.ShapeDtypeStruct((1, rows), F32),
        in_specs=[pl.BlockSpec(memory_space=pl.ANY)] * 4,
        out_specs=pl.BlockSpec(memory_space=pltpu.VMEM),
        scratch_shapes=[
            pltpu.VMEM((rows, width), BF16),
            pltpu.VMEM((1, rows), jnp.int32),
            pltpu.VMEM((1, rows), jnp.int32),
            pltpu.VMEM((1, clusters), jnp.int32),
            pltpu.VMEM((rows, width), BF16),
            pltpu.VMEM((DEVICES, SLOTS, width), BF16),
            pltpu.VMEM((DEVICES, SLOTS, width), BF16),
            pltpu.VMEM((SRC, 1, LANES), F32),
            pltpu.VMEM((SRC, 1, LANES), F32),
            pltpu.VMEM((GRP, SRC, 1, LANES), F32),
            pltpu.VMEM((CLASSES, rows, CLASS_ROWS), BF16),
            pltpu.VMEM((LANES, SRC * LANES), BF16),
            pltpu.VMEM((rows, width), F32),
            pltpu.VMEM((2, HELD, HALF, width), BF16),
            pltpu.VMEM((2, HELD, 1, HALF), F32),
            pltpu.VMEM((2, HELD, 1, HALF), jnp.int32),
            pltpu.VMEM((11, HALF // LANES, LANES), F32),
            pltpu.VMEM((GRP * 9, HALF // LANES, LANES), F32),
            pltpu.VMEM((GRP * 2, HALF // LANES, LANES), F32),
            pltpu.VMEM((GRP, rows // LANES, LANES), F32),
            pltpu.VMEM((SRC, 1, LANES), F32),
            pltpu.VMEM((SRC, 1, LANES), F32),
            pltpu.SemaphoreType.DMA((4,)),
            pltpu.SemaphoreType.REGULAR,
            pltpu.SemaphoreType.DMA((CLASSES,)),
            pltpu.SemaphoreType.DMA((CLASSES,)),
            pltpu.SemaphoreType.DMA,
            pltpu.SemaphoreType.DMA,
            pltpu.SemaphoreType.DMA,
            pltpu.SemaphoreType.DMA,
            pltpu.SemaphoreType.DMA((2, 3, 2)),
            pltpu.SemaphoreType.DMA((2, 3, 2)),
            pltpu.SemaphoreType.DMA((2,)),
            pltpu.SemaphoreType.DMA((2,)),
            pltpu.SemaphoreType.DMA((2, 2)),
            pltpu.SemaphoreType.DMA((2, 2)),
            pltpu.SemaphoreType.DMA,
            pltpu.SemaphoreType.DMA,
            pltpu.SemaphoreType.DMA,
            pltpu.SemaphoreType.DMA,
            pltpu.SemaphoreType.DMA,
            pltpu.SemaphoreType.DMA,
        ],
        compiler_params=pltpu.CompilerParams(
            collective_id=0, has_side_effects=True, vmem_limit_bytes=50 * 1024 * 1024
        ),
        name="dedup",
    )(
        embeds,
        cluster_id.reshape(1, rows),
        cluster_rank.reshape(1, rows),
        cluster_size.reshape(1, -1),
    )
    return best.reshape(rows)


def solution(mesh):
    placed = (P(("src", "grp"), None), P(("src", "grp")), P(("src", "grp")), P())
    return jax.shard_map(
        on_device, mesh=mesh, in_specs=placed, out_specs=P(("src", "grp")), check_vma=False
    )
```

```python
import jax
import jax.numpy as jnp
from jax import lax
from jax.experimental import pallas as pl
from jax.experimental.pallas import tpu as pltpu
from jax.sharding import PartitionSpec as P

MESH = pl.DeviceIdType.MESH
F32 = jnp.float32
BF16 = jnp.bfloat16

epsilon = 1e-06

DEVICES = 128
SRC = 16
GRP = 8
LANES = 128
SLOTS = 16
CLASSES = 4
PER = DEVICES // CLASSES
CLASS_ROWS = PER * SLOTS
HALF = 512
QUARTER = 256
HELD = 6
EARLY = 66
MIX, UNMIX = 91, 83

NN = (((1,), (0,)), ((), ()))
NT = (((1,), (1,)), ((), ()))


def dot(a, b, dims=NN):
    return lax.dot_general(a, b, dims, preferred_element_type=F32)


def one_hot(mask):
    return jnp.where(mask, 1.0, 0.0).astype(BF16)


def iota(shape, dim):
    return lax.broadcasted_iota(jnp.int32, shape, dim)


def three_parts(x):
    first = x.astype(BF16)
    rest = x - first.astype(F32)
    second = rest.astype(BF16)
    third = (rest - second.astype(F32)).astype(BF16)
    return first, second, third


def kernel(
    embeds_hbm,
    ids_hbm,
    ranks_hbm,
    sizes_hbm,
    out,
    embeds,
    ids,
    ranks,
    sizes,
    unit,
    send,
    recv,
    sent_meta,
    column_meta,
    group_meta,
    place_of,
    look,
    gathered,
    blocks,
    tops,
    lows,
    shares,
    early,
    late,
    best,
    answers,
    returned,
    load_sem,
    again_sem,
    send_sem,
    recv_sem,
    column_send_sem,
    column_recv_sem,
    group_send_sem,
    group_recv_sem,
    block_send_sem,
    block_recv_sem,
    peer_send_sem,
    peer_recv_sem,
    forward_send_sem,
    forward_recv_sem,
    early_send_sem,
    early_recv_sem,
    late_send_sem,
    late_recv_sem,
    answer_send_sem,
    answer_recv_sem,
):
    rows, width = embeds.shape
    src = lax.axis_index("src")
    grp = lax.axis_index("grp")
    x, y = src >> 2, src & 3
    z, core = grp >> 1, grp & 1

    def src_at(n, sign):
        return ((x + sign * (n >> 2)) & 3) * 4 + ((y + sign * n) & 3)

    def grp_at(m, sign):
        return ((z + sign * (m >> 1)) & 3) * 2 + ((core + m) & 1)

    barrier = pltpu.get_barrier_semaphore()

    def greet_src(n, carry):
        pl.semaphore_signal(barrier, inc=1, device_id=(src_at(n, 1), grp), device_id_type=MESH)
        return carry

    def greet_grp(m, carry):
        pl.semaphore_signal(barrier, inc=1, device_id=(src, grp_at(m, 1)), device_id_type=MESH)
        return carry

    lax.fori_loop(1, SRC, greet_src, 0)
    lax.fori_loop(1, GRP, greet_grp, 0)

    loads = []
    for n, (source, target) in enumerate(
        ((ids_hbm, ids), (ranks_hbm, ranks), (sizes_hbm, sizes), (embeds_hbm, embeds))
    ):
        copy = pltpu.make_async_copy(source, target, load_sem.at[n])
        copy.start()
        loads.append(copy)

    for copy in loads[:3]:
        copy.wait()
    clusters = sizes.shape[1]
    size_row = sizes[...].astype(F32)
    earlier = iota((clusters, clusters), 1) < iota((clusters, clusters), 0)
    starts = jnp.sum(jnp.where(earlier, size_row, 0.0), axis=1, keepdims=True)
    mine = iota((clusters, rows), 0) == ids[...]
    start_row = jnp.sum(jnp.where(mine, starts, 0.0), axis=0, keepdims=True)
    position = start_row.astype(jnp.int32) + ranks[...]
    tiling = position >> 16
    to_x = (((position >> 15) & 1) * 2 + ((position >> 12) & 1) - tiling) & 3
    to_y = (((position >> 14) & 1) * 2 + ((position >> 11) & 1) - tiling) & 3
    to_z = (((position >> 13) & 1) * 2 + ((position >> 10) & 1) - tiling) & 3
    to_core = (position >> 9) & 1
    to_grp = to_z * 2 + to_core
    dx, dy, dz = (to_x - x) & 3, (to_y - y) & 3, (to_z - z) & 3
    dc = (to_core - core) & 1
    column_row = dx * 4 + dy
    step_row = ((column_row * GRP + dz * 2 + dc) * UNMIX) & (DEVICES - 1)
    to_step = one_hot(iota((DEVICES, rows), 0) == step_row)
    to_column = one_hot(iota((SRC, rows), 0) == column_row)

    part = 256
    before = one_hot(iota((part, part), 0) < iota((part, part), 1))
    carry = jnp.zeros((DEVICES, 1), F32)
    slot_parts = []
    for n in range(rows // part):
        piece = to_step[:, n * part : (n + 1) * part]
        piece32 = piece.astype(F32)
        count = dot(piece, before) + carry
        slot_parts.append(jnp.sum(piece32 * count, axis=0, keepdims=True))
        carry = carry + jnp.sum(piece32, axis=1, keepdims=True)
    slot_row = jnp.concatenate(slot_parts, axis=1).astype(jnp.int32)
    index_row = step_row * SLOTS + slot_row
    lane_hot = one_hot(iota((LANES, rows), 0) == to_grp * SLOTS + slot_row)

    place_row = tiling * HALF + (position & (HALF - 1)) + 1
    upper = to_column * (place_row >> 3).astype(F32).astype(BF16)
    lower = to_column * (place_row & 7).astype(F32).astype(BF16)
    meta = 8.0 * dot(upper, lane_hot, NT) + dot(lower, lane_hot, NT)
    for n in range(SRC):
        sent_meta[n] = meta[n : n + 1, :]
    column_meta[0] = sent_meta[0]

    pl.semaphore_wait(barrier, SRC - 1 + GRP - 1)

    def greet_again(m, carry):
        pl.semaphore_signal(again_sem, inc=1, device_id=(src, grp_at(m, 1)), device_id_type=MESH)
        return carry

    lax.fori_loop(1, GRP, greet_again, 0)

    def send_column_meta(n, carry):
        pltpu.make_async_remote_copy(
            src_ref=sent_meta.at[n],
            dst_ref=column_meta.at[n],
            send_sem=column_send_sem,
            recv_sem=column_recv_sem,
            device_id=(src_at(n, 1), grp),
            device_id_type=MESH,
        ).start()
        return carry

    lax.fori_loop(1, SRC, send_column_meta, 0)

    loads[3].wait()

    def normalise(n, carry):
        here = pl.ds(pl.multiple_of(n * part, part), part)
        wide = embeds[here, :].astype(F32)
        total = jnp.sum(wide * wide, axis=1, keepdims=True)
        unit[here, :] = (wide * lax.rsqrt(total + epsilon)).astype(BF16)
        return carry

    lax.fori_loop(0, rows // part, normalise, 0)

    def wait_all(ref, sem, count):
        pltpu.make_async_copy(ref.at[pl.ds(1, count)], ref.at[pl.ds(1, count)], sem).wait()

    for n in range(CLASSES):
        pick = one_hot(iota((CLASS_ROWS, rows), 0) + n * CLASS_ROWS == index_row)
        packed = dot(pick, unit[...]).astype(BF16)
        send[pl.ds(n * PER, PER)] = packed.reshape(PER, SLOTS, width)
        if n == 0:
            recv[0] = send[0]
            pl.semaphore_wait(again_sem, GRP - 1)

        def send_step(step, carry):
            k = (step * MIX) & (DEVICES - 1)
            pltpu.make_async_remote_copy(
                src_ref=send.at[step],
                dst_ref=recv.at[step],
                send_sem=send_sem.at[n],
                recv_sem=recv_sem.at[n],
                device_id=(src_at(k >> 3, 1), grp_at(k & 7, 1)),
                device_id_type=MESH,
            ).start()
            return carry

        lax.fori_loop(max(1, n * PER), (n + 1) * PER, send_step, 0)

        if n == 0:
            wait_all(column_meta, column_recv_sem, SRC - 1)
            group_meta[0] = column_meta[...]

            def send_group_meta(m, carry):
                pltpu.make_async_remote_copy(
                    src_ref=column_meta,
                    dst_ref=group_meta.at[m],
                    send_sem=group_send_sem,
                    recv_sem=group_recv_sem,
                    device_id=(src, grp_at(m, 1)),
                    device_id_type=MESH,
                ).start()
                return carry

            lax.fori_loop(1, GRP, send_group_meta, 0)

    lane_no = iota((1, LANES), 1)
    pick_rows = []
    for n in range(SRC):
        wanted = column_meta[n].astype(jnp.int32) - 1
        look[:, n * LANES : (n + 1) * LANES] = one_hot(iota((LANES, LANES), 0) == (wanted & 127))
        row_no = (lane_no // SLOTS) * 8 + (wanted >> 7)
        pick_rows.append(jnp.where(wanted >= 0, row_no, -1))
    pick_row = jnp.concatenate(pick_rows, axis=1)

    wait_all(group_meta, group_recv_sem, GRP - 1)

    all_meta = group_meta[...].reshape(DEVICES, LANES).astype(jnp.int32)
    choose = one_hot(iota((LANES, LANES), 0) == grp * SLOTS + (iota((LANES, LANES), 1) & 15))
    number = iota((DEVICES, LANES), 0)
    step_of = (((number & 15) * GRP + (number >> 4)) * UNMIX) & (DEVICES - 1)
    kept = (iota((DEVICES, LANES), 1) >> 4) == (step_of & 7)
    number = iota((SRC, DEVICES), 1)
    step_of = (((number & 15) * GRP + (number >> 4)) * UNMIX) & (DEVICES - 1)
    line_hot = one_hot((step_of >> 3) == iota((SRC, DEVICES), 0))
    got_places = jnp.zeros((SRC, LANES), F32)
    for scale, digit in ((8.0, all_meta >> 3), (1.0, all_meta & 7)):
        spread = dot(digit.astype(F32).astype(BF16), choose)
        spread = jnp.where(kept, spread, 0.0).astype(BF16)
        got_places += scale * dot(line_hot, spread)
    got_places = got_places.astype(jnp.int32)

    for n in range(CLASSES):
        for m in range(CLASS_ROWS // LANES):
            line = n * (CLASS_ROWS // LANES) + m
            hit = iota((rows, LANES), 0) + 1 == got_places[line : line + 1, :]
            place_of[n, :, m * LANES : (m + 1) * LANES] = one_hot(hit)

    def bits(tiling):
        return (x + tiling) & 1, (y + tiling) & 1, (z + tiling) & 1

    def across(tiling, *axes):
        place = [x, y, z]
        for axis in axes:
            place[axis] = (place[axis] + 1 - 2 * bits(tiling)[axis]) & 3
        return place

    def device_across(tiling, axes, to_core):
        to_x, to_y, to_z = across(tiling, *axes)
        return (to_x * 4 + to_y, to_z * 2 + to_core)

    def number(tiling, slot):
        v1, v2, v3 = bits(tiling)
        if not isinstance(slot, int) or slot < 2:
            own = slot
        elif slot == 2:
            v1, own = 1 - v1, core ^ v1
        elif slot == 3:
            v2, own = 1 - v2, core
        elif slot == 4:
            v3, own = 1 - v3, core ^ v2
        else:
            v2, v3, own = 1 - v2, 1 - v3, core
        return ((v1 * 2 + v2) * 2 + v3) * 2 + own

    def base(tiling):
        cube_x, cube_y, cube_z = (((i + tiling) & 3) >> 1 for i in (x, y, z))
        return (tiling * 8 + cube_x * 4 + cube_y * 2 + cube_z) * (GRP * rows)

    for tiling in range(2):
        for slot in range(HELD):
            places = number(tiling, slot) * HALF + base(tiling) + iota((1, HALF), 1)
            below = jnp.where(starts <= places.astype(F32), starts, 0.0)
            low = jnp.max(below, axis=0, keepdims=True)
            lows[tiling, slot] = low.astype(jnp.int32) - base(tiling)
            tops[tiling, slot] = jnp.full((1, HALF), -1.0, F32)

    def first_half(axis):
        return 1 if axis == 1 else 0

    def neighbour_copy(tiling, axis, half):
        v1, v2, v3 = bits(tiling)
        to_core = core ^ (1 - v1, 0, v2)[axis]
        here = pl.ds(half * QUARTER, QUARTER)
        return pltpu.make_async_remote_copy(
            src_ref=blocks.at[tiling, core, here],
            dst_ref=blocks.at[tiling, 2 + axis, here],
            send_sem=block_send_sem.at[tiling, axis, half],
            recv_sem=block_recv_sem.at[tiling, axis, half],
            device_id=device_across(tiling, (axis,), to_core),
            device_id_type=MESH,
        )

    def peer_copy(tiling):
        return pltpu.make_async_remote_copy(
            src_ref=blocks.at[tiling, core],
            dst_ref=blocks.at[tiling, core],
            send_sem=peer_send_sem.at[tiling],
            recv_sem=peer_recv_sem.at[tiling],
            device_id=(src, z * 2 + core ^ 1),
            device_id_type=MESH,
        )

    def forward_copy(tiling, axis):
        half = first_half(axis)
        here = pl.ds(half * QUARTER, QUARTER)
        to_core = core if axis == 1 else core ^ bits(tiling)[1]
        return pltpu.make_async_remote_copy(
            src_ref=blocks.at[tiling, 2 + axis, here],
            dst_ref=blocks.at[tiling, 5, here],
            send_sem=forward_send_sem.at[tiling, half],
            recv_sem=forward_recv_sem.at[tiling, half],
            device_id=device_across(tiling, (3 - axis,), to_core),
            device_id_type=MESH,
        )

    for n in range(CLASSES):
        first = 1 if n == 0 else 0
        group = recv.at[pl.ds(n * PER + first, PER - first)]
        pltpu.make_async_copy(group, group, recv_sem.at[n]).wait()
        arrived = recv[pl.ds(n * PER, PER)].reshape(CLASS_ROWS, width)
        for tiling in range(2):
            here = pl.ds(tiling * HALF, HALF)
            found = dot(place_of[n, here, :], arrived)
            if n == 0:
                gathered[here, :] = found
            elif n < CLASSES - 1:
                gathered[here, :] += found
            else:
                blocks[tiling, core] = (gathered[here, :] + found).astype(BF16)
                for axis in range(3):
                    neighbour_copy(tiling, axis, first_half(axis)).start()
                peer_copy(tiling).start()
                for axis in range(3):
                    neighbour_copy(tiling, axis, 1 - first_half(axis)).start()

    def score(tiling, key, query, same=False):
        key_slot, key_start, keys = key[:3]
        query_slot, query_start, queries = query[:3]
        products = dot(
            blocks[tiling, key_slot, pl.ds(key_start, keys), :],
            blocks[tiling, query_slot, pl.ds(query_start, queries), :],
            NT,
        )
        columns = slice(query_start, query_start + queries)
        key_no = iota((keys, queries), 0) + key_start
        allowed = key_no >= lows[tiling, query_slot][:, columns] - key[3] * HALF
        if same:
            allowed = allowed & (key_no < iota((keys, queries), 1) + query_start)
        found = jnp.max(jnp.where(allowed, products, -1.0), axis=0, keepdims=True)
        tops[tiling, query_slot, :, columns] = jnp.maximum(
            tops[tiling, query_slot, :, columns], found
        )

    def pair(tiling, a, b):
        a, b = (*a, number(tiling, a[0])), (*b, number(tiling, b[0]))
        a_first = a[3] < b[3]

        @pl.when(a_first)
        def _():
            score(tiling, a, b)

        @pl.when(jnp.logical_not(a_first))
        def _():
            score(tiling, b, a)

    def own_slot(tiling, axis):
        v1, v2, v3 = bits(tiling)
        return core ^ (0, v2, v2 ^ v3)[axis]

    def own_scores(tiling, carry):
        mine = (core, 0, HALF, number(tiling, core))
        score(tiling, mine, mine, True)
        peer = blocks.at[tiling, core ^ 1]
        pltpu.make_async_copy(peer, peer, peer_recv_sem.at[tiling]).wait()
        start = pl.multiple_of(core * QUARTER, QUARTER)
        key = (0, start, QUARTER, number(tiling, 0))
        score(tiling, key, (1, 0, HALF, number(tiling, 1)))
        return carry

    lax.fori_loop(0, 2, own_scores, 0)

    def wait_neighbour(tiling, axis, half):
        here = blocks.at[tiling, 2 + axis, pl.ds(half * QUARTER, QUARTER)]
        pltpu.make_async_copy(here, here, block_recv_sem.at[tiling, axis, half]).wait()

    def forward(tiling, carry):
        for axis in (1, 2):
            wait_neighbour(tiling, axis, first_half(axis))
            forward_copy(tiling, axis).start()
        return carry

    lax.fori_loop(0, 2, forward, 0)

    def held_part(axis, half):
        return (2 + axis, half * QUARTER, QUARTER)

    def first_scores(tiling, carry):
        wait_neighbour(tiling, 0, first_half(0))
        for axis in range(3):
            own = (own_slot(tiling, axis), 0, HALF)
            pair(tiling, own, held_part(axis, first_half(axis)))
        for axis, other in ((0, 1), (0, 2), (1, 2)):
            pair(
                tiling, held_part(axis, first_half(axis)), held_part(other, first_half(other))
            )
        return carry

    lax.fori_loop(0, 2, first_scores, 0)

    def second_scores(tiling, carry):
        for axis in range(3):
            wait_neighbour(tiling, axis, 1 - first_half(axis))
            own = (own_slot(tiling, axis), 0, HALF)
            pair(tiling, own, held_part(axis, 1 - first_half(axis)))
        for axis, other in ((0, 1), (0, 2), (1, 2)):
            pair(tiling, held_part(axis, 1 - first_half(axis)), (2 + other, 0, HALF))
            pair(
                tiling,
                held_part(axis, first_half(axis)),
                held_part(other, 1 - first_half(other)),
            )
        return carry

    lax.fori_loop(0, 2, second_scores, 0)

    zero_tiling = x & 1
    one_tiling = 1 - zero_tiling

    def stage(line, slot, tiling):
        for n in range(HALF // LANES):
            shares[line, n : n + 1, :] = tops[tiling, slot, :, n * LANES : (n + 1) * LANES]

    def send_found(line, target, owner, to_all, send_sem, recv_sem):
        source = shares.at[line]
        if line < 9:
            place = early.at[owner * 9 + line]
        else:
            place = late.at[owner * 2 + line - 9]

        def send_one(m, carry):
            pltpu.make_async_remote_copy(
                src_ref=source,
                dst_ref=place,
                send_sem=send_sem,
                recv_sem=recv_sem,
                device_id=(target, grp_at(m, 1)),
                device_id_type=MESH,
            ).start()
            return carry

        lax.fori_loop(0 if to_all else 1, GRP, send_one, 0)
        if not to_all:
            place[...] = source[...]

    for tiling in range(2):
        v2 = bits(tiling)[1]
        for kind, slot in enumerate((core, core ^ 1, 3, 4)):
            stage(tiling * 4 + kind, slot, tiling)
        line = tiling * 4
        send_found(line, src, grp, False, early_send_sem, early_recv_sem)
        send_found(line + 1, src, grp ^ 1, False, early_send_sem, early_recv_sem)
        target, owner = device_across(tiling, (1,), core)
        send_found(line + 2, target, owner, True, early_send_sem, early_recv_sem)
        target, owner = device_across(tiling, (2,), core ^ v2)
        send_found(line + 3, src, owner, False, early_send_sem, early_recv_sem)
    stage(8, 2, one_tiling)
    target, owner = device_across(one_tiling, (0,), core ^ 1)
    send_found(8, target, owner, True, early_send_sem, early_recv_sem)

    def far_scores(tiling, carry):
        for half in range(2):
            here = blocks.at[tiling, 5, pl.ds(half * QUARTER, QUARTER)]
            pltpu.make_async_copy(here, here, forward_recv_sem.at[tiling, half]).wait()
            pair(tiling, (2, 0, HALF), (5, half * QUARTER, QUARTER))
        return carry

    lax.fori_loop(0, 2, far_scores, 0)

    stage(9, 2, zero_tiling)
    target, owner = device_across(zero_tiling, (0,), core)
    send_found(9, target, owner, True, late_send_sem, late_recv_sem)
    stage(10, 5, one_tiling)
    target, owner = device_across(one_tiling, (1, 2), core)
    send_found(10, target, owner, True, late_send_sem, late_recv_sem)

    def wait_early(sem):
        here = early.at[pl.ds(0, EARLY)]
        pltpu.make_async_copy(here, here, sem).wait()

    wait_early(early_recv_sem)
    for owner in range(GRP):
        for tiling in range(2):
            line = owner * 9 + tiling * 4
            early[line] = jnp.maximum(
                jnp.maximum(early[line], early[line + 1]),
                jnp.maximum(early[line + 2], early[line + 3]),
            )
    pltpu.make_async_copy(late, late, late_recv_sem).wait()
    for owner in range(GRP):
        line = owner * 9
        to_zero, to_one = early[line + 8], jnp.maximum(late[owner * 2], late[owner * 2 + 1])
        added = (
            jnp.maximum(early[line], jnp.where(zero_tiling == 0, to_zero, to_one)),
            jnp.maximum(early[line + 4], jnp.where(zero_tiling == 0, to_one, to_zero)),
        )
        best[owner] = jnp.concatenate(added, axis=0)

    lines = GRP * rows // LANES
    parts = jnp.concatenate(three_parts(best[...].reshape(lines, LANES)), axis=0)
    answer = dot(parts, look[...])
    answer = answer[:lines] + answer[lines : 2 * lines] + answer[2 * lines :]
    right = iota(answer.shape, 0) == pick_row
    answer = jnp.sum(jnp.where(right, answer, 0.0), axis=0, keepdims=True)
    for n in range(SRC):
        answers[n] = answer[:, n * LANES : (n + 1) * LANES]
    returned[0] = answers[0]

    def send_answer(n, carry):
        pltpu.make_async_remote_copy(
            src_ref=answers.at[n],
            dst_ref=returned.at[n],
            send_sem=answer_send_sem,
            recv_sem=answer_recv_sem,
            device_id=(src_at(n, -1), grp),
            device_id_type=MESH,
        ).start()
        return carry

    lax.fori_loop(1, SRC, send_answer, 0)
    wait_all(returned, answer_recv_sem, SRC - 1)
    table = returned[...].reshape(SRC, LANES).T
    parts = jnp.concatenate(three_parts(table), axis=1)
    chosen = dot(parts, jnp.concatenate([to_column] * 3, axis=0))
    out[...] = jnp.sum(chosen * lane_hot.astype(F32), axis=0, keepdims=True)

    wait_all(sent_meta, column_send_sem, SRC - 1)
    wait_all(group_meta, group_send_sem, GRP - 1)
    wait_early(early_send_sem)
    pltpu.make_async_copy(late, late, late_send_sem).wait()
    wait_all(answers, answer_send_sem, SRC - 1)
    for n in range(CLASSES):
        first = 1 if n == 0 else 0
        group = send.at[pl.ds(n * PER + first, PER - first)]
        pltpu.make_async_copy(group, group, send_sem.at[n]).wait()
    for tiling in range(2):
        whole = blocks.at[tiling, core]
        pltpu.make_async_copy(whole, whole, peer_send_sem.at[tiling]).wait()
        for half in range(2):
            here = blocks.at[tiling, core, pl.ds(half * QUARTER, QUARTER)]
            for axis in range(3):
                pltpu.make_async_copy(here, here, block_send_sem.at[tiling, axis, half]).wait()
            pltpu.make_async_copy(here, here, forward_send_sem.at[tiling, half]).wait()


def on_device(embeds, cluster_id, cluster_rank, cluster_size):
    rows, width = embeds.shape
    clusters = cluster_size.shape[0]
    best = pl.pallas_call(
        kernel,
        out_shape=jax.ShapeDtypeStruct((1, rows), F32),
        in_specs=[pl.BlockSpec(memory_space=pl.ANY)] * 4,
        out_specs=pl.BlockSpec(memory_space=pltpu.VMEM),
        scratch_shapes=[
            pltpu.VMEM((rows, width), BF16),
            pltpu.VMEM((1, rows), jnp.int32),
            pltpu.VMEM((1, rows), jnp.int32),
            pltpu.VMEM((1, clusters), jnp.int32),
            pltpu.VMEM((rows, width), BF16),
            pltpu.VMEM((DEVICES, SLOTS, width), BF16),
            pltpu.VMEM((DEVICES, SLOTS, width), BF16),
            pltpu.VMEM((SRC, 1, LANES), F32),
            pltpu.VMEM((SRC, 1, LANES), F32),
            pltpu.VMEM((GRP, SRC, 1, LANES), F32),
            pltpu.VMEM((CLASSES, rows, CLASS_ROWS), BF16),
            pltpu.VMEM((LANES, SRC * LANES), BF16),
            pltpu.VMEM((rows, width), F32),
            pltpu.VMEM((2, HELD, HALF, width), BF16),
            pltpu.VMEM((2, HELD, 1, HALF), F32),
            pltpu.VMEM((2, HELD, 1, HALF), jnp.int32),
            pltpu.VMEM((11, HALF // LANES, LANES), F32),
            pltpu.VMEM((GRP * 9, HALF // LANES, LANES), F32),
            pltpu.VMEM((GRP * 2, HALF // LANES, LANES), F32),
            pltpu.VMEM((GRP, rows // LANES, LANES), F32),
            pltpu.VMEM((SRC, 1, LANES), F32),
            pltpu.VMEM((SRC, 1, LANES), F32),
            pltpu.SemaphoreType.DMA((4,)),
            pltpu.SemaphoreType.REGULAR,
            pltpu.SemaphoreType.DMA((CLASSES,)),
            pltpu.SemaphoreType.DMA((CLASSES,)),
            pltpu.SemaphoreType.DMA,
            pltpu.SemaphoreType.DMA,
            pltpu.SemaphoreType.DMA,
            pltpu.SemaphoreType.DMA,
            pltpu.SemaphoreType.DMA((2, 3, 2)),
            pltpu.SemaphoreType.DMA((2, 3, 2)),
            pltpu.SemaphoreType.DMA((2,)),
            pltpu.SemaphoreType.DMA((2,)),
            pltpu.SemaphoreType.DMA((2, 2)),
            pltpu.SemaphoreType.DMA((2, 2)),
            pltpu.SemaphoreType.DMA,
            pltpu.SemaphoreType.DMA,
            pltpu.SemaphoreType.DMA,
            pltpu.SemaphoreType.DMA,
            pltpu.SemaphoreType.DMA,
            pltpu.SemaphoreType.DMA,
        ],
        compiler_params=pltpu.CompilerParams(
            collective_id=0, has_side_effects=True, vmem_limit_bytes=50 * 1024 * 1024
        ),
        name="dedup",
    )(
        embeds,
        cluster_id.reshape(1, rows),
        cluster_rank.reshape(1, rows),
        cluster_size.reshape(1, -1),
    )
    return best.reshape(rows)


def solution(mesh):
    placed = (P(("src", "grp"), None), P(("src", "grp")), P(("src", "grp")), P())
    return jax.shard_map(
        on_device, mesh=mesh, in_specs=placed, out_specs=P(("src", "grp")), check_vma=False
    )
```

```python
import jax
import jax.numpy as jnp
from jax import lax
from jax.experimental import pallas as pl
from jax.experimental.pallas import tpu as pltpu
from jax.sharding import PartitionSpec as P

MESH = pl.DeviceIdType.MESH
F32 = jnp.float32
BF16 = jnp.bfloat16

epsilon = 1e-06

DEVICES = 128
SRC = 16
GRP = 8
LANES = 128
SLOTS = 16
CLASSES = 4
PER = DEVICES // CLASSES
CLASS_ROWS = PER * SLOTS
HALF = 512
QUARTER = 256
HELD = 6
EARLY = 66
MIX, UNMIX = 91, 83

NN = (((1,), (0,)), ((), ()))
NT = (((1,), (1,)), ((), ()))


def dot(a, b, dims=NN):
    return lax.dot_general(a, b, dims, preferred_element_type=F32)


def one_hot(mask):
    return jnp.where(mask, 1.0, 0.0).astype(BF16)


def iota(shape, dim):
    return lax.broadcasted_iota(jnp.int32, shape, dim)


def three_parts(x):
    first = x.astype(BF16)
    rest = x - first.astype(F32)
    second = rest.astype(BF16)
    third = (rest - second.astype(F32)).astype(BF16)
    return first, second, third


def kernel(
    embeds_hbm,
    ids_hbm,
    ranks_hbm,
    sizes_hbm,
    out,
    embeds,
    ids,
    ranks,
    sizes,
    unit,
    send,
    recv,
    sent_meta,
    column_meta,
    group_meta,
    place_of,
    look,
    gathered,
    blocks,
    tops,
    lows,
    shares,
    early,
    late,
    best,
    answers,
    returned,
    load_sem,
    again_sem,
    send_sem,
    recv_sem,
    column_send_sem,
    column_recv_sem,
    group_send_sem,
    group_recv_sem,
    block_send_sem,
    block_recv_sem,
    peer_send_sem,
    peer_recv_sem,
    forward_send_sem,
    forward_recv_sem,
    early_send_sem,
    early_recv_sem,
    late_send_sem,
    late_recv_sem,
    answer_send_sem,
    answer_recv_sem,
):
    rows, width = embeds.shape
    src = lax.axis_index("src")
    grp = lax.axis_index("grp")
    x, y = src >> 2, src & 3
    z, core = grp >> 1, grp & 1

    def src_at(n, sign):
        return ((x + sign * (n >> 2)) & 3) * 4 + ((y + sign * n) & 3)

    def grp_at(m, sign):
        return ((z + sign * (m >> 1)) & 3) * 2 + ((core + m) & 1)

    barrier = pltpu.get_barrier_semaphore()

    def greet_src(n, carry):
        pl.semaphore_signal(barrier, inc=1, device_id=(src_at(n, 1), grp), device_id_type=MESH)
        return carry

    def greet_grp(m, carry):
        pl.semaphore_signal(barrier, inc=1, device_id=(src, grp_at(m, 1)), device_id_type=MESH)
        return carry

    lax.fori_loop(1, SRC, greet_src, 0)
    lax.fori_loop(1, GRP, greet_grp, 0)

    loads = []
    for n, (source, target) in enumerate(
        ((ids_hbm, ids), (ranks_hbm, ranks), (sizes_hbm, sizes), (embeds_hbm, embeds))
    ):
        copy = pltpu.make_async_copy(source, target, load_sem.at[n])
        copy.start()
        loads.append(copy)

    for copy in loads[:3]:
        copy.wait()
    clusters = sizes.shape[1]
    size_row = sizes[...].astype(F32)
    earlier = iota((clusters, clusters), 1) < iota((clusters, clusters), 0)
    starts = jnp.sum(jnp.where(earlier, size_row, 0.0), axis=1, keepdims=True)
    mine = iota((clusters, rows), 0) == ids[...]
    start_row = jnp.sum(jnp.where(mine, starts, 0.0), axis=0, keepdims=True)
    position = start_row.astype(jnp.int32) + ranks[...]
    tiling = position >> 16
    to_x = (((position >> 15) & 1) * 2 + ((position >> 12) & 1) - tiling) & 3
    to_y = (((position >> 14) & 1) * 2 + ((position >> 11) & 1) - tiling) & 3
    to_z = (((position >> 13) & 1) * 2 + ((position >> 10) & 1) - tiling) & 3
    to_core = (position >> 9) & 1
    to_grp = to_z * 2 + to_core
    dx, dy, dz = (to_x - x) & 3, (to_y - y) & 3, (to_z - z) & 3
    dc = (to_core - core) & 1
    column_row = dx * 4 + dy
    step_row = ((column_row * GRP + dz * 2 + dc) * UNMIX) & (DEVICES - 1)
    to_step = one_hot(iota((DEVICES, rows), 0) == step_row)
    to_column = one_hot(iota((SRC, rows), 0) == column_row)

    part = 256
    before = one_hot(iota((part, part), 0) < iota((part, part), 1))
    carry = jnp.zeros((DEVICES, 1), F32)
    slot_parts = []
    for n in range(rows // part):
        piece = to_step[:, n * part : (n + 1) * part]
        piece32 = piece.astype(F32)
        count = dot(piece, before) + carry
        slot_parts.append(jnp.sum(piece32 * count, axis=0, keepdims=True))
        carry = carry + jnp.sum(piece32, axis=1, keepdims=True)
    slot_row = jnp.concatenate(slot_parts, axis=1).astype(jnp.int32)
    index_row = step_row * SLOTS + slot_row
    lane_hot = one_hot(iota((LANES, rows), 0) == to_grp * SLOTS + slot_row)

    place_row = tiling * HALF + (position & (HALF - 1)) + 1
    upper = to_column * (place_row >> 3).astype(F32).astype(BF16)
    lower = to_column * (place_row & 7).astype(F32).astype(BF16)
    meta = 8.0 * dot(upper, lane_hot, NT) + dot(lower, lane_hot, NT)
    for n in range(SRC):
        sent_meta[n] = meta[n : n + 1, :]
    column_meta[0] = sent_meta[0]

    loads[3].wait()

    def normalise(n, carry):
        here = pl.ds(pl.multiple_of(n * part, part), part)
        wide = embeds[here, :].astype(F32)
        total = jnp.sum(wide * wide, axis=1, keepdims=True)
        unit[here, :] = (wide * lax.rsqrt(total + epsilon)).astype(BF16)
        return carry

    lax.fori_loop(0, rows // part, normalise, 0)

    pl.semaphore_wait(barrier, SRC - 1 + GRP - 1)

    def greet_again(m, carry):
        pl.semaphore_signal(again_sem, inc=1, device_id=(src, grp_at(m, 1)), device_id_type=MESH)
        return carry

    lax.fori_loop(1, GRP, greet_again, 0)

    def send_column_meta(n, carry):
        pltpu.make_async_remote_copy(
            src_ref=sent_meta.at[n],
            dst_ref=column_meta.at[n],
            send_sem=column_send_sem,
            recv_sem=column_recv_sem,
            device_id=(src_at(n, 1), grp),
            device_id_type=MESH,
        ).start()
        return carry

    lax.fori_loop(1, SRC, send_column_meta, 0)

    def wait_all(ref, sem, count):
        pltpu.make_async_copy(ref.at[pl.ds(1, count)], ref.at[pl.ds(1, count)], sem).wait()

    for n in range(CLASSES):
        pick = one_hot(iota((CLASS_ROWS, rows), 0) + n * CLASS_ROWS == index_row)
        packed = dot(pick, unit[...]).astype(BF16)
        send[pl.ds(n * PER, PER)] = packed.reshape(PER, SLOTS, width)
        if n == 0:
            recv[0] = send[0]
            pl.semaphore_wait(again_sem, GRP - 1)

        def send_step(step, carry):
            k = (step * MIX) & (DEVICES - 1)
            pltpu.make_async_remote_copy(
                src_ref=send.at[step],
                dst_ref=recv.at[step],
                send_sem=send_sem.at[n],
                recv_sem=recv_sem.at[n],
                device_id=(src_at(k >> 3, 1), grp_at(k & 7, 1)),
                device_id_type=MESH,
            ).start()
            return carry

        lax.fori_loop(max(1, n * PER), (n + 1) * PER, send_step, 0)

        if n == 0:
            wait_all(column_meta, column_recv_sem, SRC - 1)
            group_meta[0] = column_meta[...]

            def send_group_meta(m, carry):
                pltpu.make_async_remote_copy(
                    src_ref=column_meta,
                    dst_ref=group_meta.at[m],
                    send_sem=group_send_sem,
                    recv_sem=group_recv_sem,
                    device_id=(src, grp_at(m, 1)),
                    device_id_type=MESH,
                ).start()
                return carry

            lax.fori_loop(1, GRP, send_group_meta, 0)

    lane_no = iota((1, LANES), 1)
    pick_rows = []
    for n in range(SRC):
        wanted = column_meta[n].astype(jnp.int32) - 1
        look[:, n * LANES : (n + 1) * LANES] = one_hot(iota((LANES, LANES), 0) == (wanted & 127))
        row_no = (lane_no // SLOTS) * 8 + (wanted >> 7)
        pick_rows.append(jnp.where(wanted >= 0, row_no, -1))
    pick_row = jnp.concatenate(pick_rows, axis=1)

    wait_all(group_meta, group_recv_sem, GRP - 1)

    all_meta = group_meta[...].reshape(DEVICES, LANES).astype(jnp.int32)
    choose = one_hot(iota((LANES, LANES), 0) == grp * SLOTS + (iota((LANES, LANES), 1) & 15))
    number = iota((DEVICES, LANES), 0)
    step_of = (((number & 15) * GRP + (number >> 4)) * UNMIX) & (DEVICES - 1)
    kept = (iota((DEVICES, LANES), 1) >> 4) == (step_of & 7)
    number = iota((SRC, DEVICES), 1)
    step_of = (((number & 15) * GRP + (number >> 4)) * UNMIX) & (DEVICES - 1)
    line_hot = one_hot((step_of >> 3) == iota((SRC, DEVICES), 0))
    got_places = jnp.zeros((SRC, LANES), F32)
    for scale, digit in ((8.0, all_meta >> 3), (1.0, all_meta & 7)):
        spread = dot(digit.astype(F32).astype(BF16), choose)
        spread = jnp.where(kept, spread, 0.0).astype(BF16)
        got_places += scale * dot(line_hot, spread)
    got_places = got_places.astype(jnp.int32)

    for n in range(CLASSES):
        for m in range(CLASS_ROWS // LANES):
            line = n * (CLASS_ROWS // LANES) + m
            hit = iota((rows, LANES), 0) + 1 == got_places[line : line + 1, :]
            place_of[n, :, m * LANES : (m + 1) * LANES] = one_hot(hit)

    def bits(tiling):
        return (x + tiling) & 1, (y + tiling) & 1, (z + tiling) & 1

    def across(tiling, *axes):
        place = [x, y, z]
        for axis in axes:
            place[axis] = (place[axis] + 1 - 2 * bits(tiling)[axis]) & 3
        return place

    def device_across(tiling, axes, to_core):
        to_x, to_y, to_z = across(tiling, *axes)
        return (to_x * 4 + to_y, to_z * 2 + to_core)

    def number(tiling, slot):
        v1, v2, v3 = bits(tiling)
        if not isinstance(slot, int) or slot < 2:
            own = slot
        elif slot == 2:
            v1, own = 1 - v1, core ^ v1
        elif slot == 3:
            v2, own = 1 - v2, core
        elif slot == 4:
            v3, own = 1 - v3, core ^ v2
        else:
            v2, v3, own = 1 - v2, 1 - v3, core
        return ((v1 * 2 + v2) * 2 + v3) * 2 + own

    def base(tiling):
        cube_x, cube_y, cube_z = (((i + tiling) & 3) >> 1 for i in (x, y, z))
        return (tiling * 8 + cube_x * 4 + cube_y * 2 + cube_z) * (GRP * rows)

    for tiling in range(2):
        for slot in range(HELD):
            places = number(tiling, slot) * HALF + base(tiling) + iota((1, HALF), 1)
            below = jnp.where(starts <= places.astype(F32), starts, 0.0)
            low = jnp.max(below, axis=0, keepdims=True)
            lows[tiling, slot] = low.astype(jnp.int32) - base(tiling)
            tops[tiling, slot] = jnp.full((1, HALF), -1.0, F32)

    def first_half(axis):
        return 1 if axis == 1 else 0

    def neighbour_copy(tiling, axis, half):
        v1, v2, v3 = bits(tiling)
        to_core = core ^ (1 - v1, 0, v2)[axis]
        here = pl.ds(half * QUARTER, QUARTER)
        return pltpu.make_async_remote_copy(
            src_ref=blocks.at[tiling, core, here],
            dst_ref=blocks.at[tiling, 2 + axis, here],
            send_sem=block_send_sem.at[tiling, axis, half],
            recv_sem=block_recv_sem.at[tiling, axis, half],
            device_id=device_across(tiling, (axis,), to_core),
            device_id_type=MESH,
        )

    def peer_copy(tiling):
        return pltpu.make_async_remote_copy(
            src_ref=blocks.at[tiling, core],
            dst_ref=blocks.at[tiling, core],
            send_sem=peer_send_sem.at[tiling],
            recv_sem=peer_recv_sem.at[tiling],
            device_id=(src, z * 2 + core ^ 1),
            device_id_type=MESH,
        )

    def forward_copy(tiling, axis):
        half = first_half(axis)
        here = pl.ds(half * QUARTER, QUARTER)
        to_core = core if axis == 1 else core ^ bits(tiling)[1]
        return pltpu.make_async_remote_copy(
            src_ref=blocks.at[tiling, 2 + axis, here],
            dst_ref=blocks.at[tiling, 5, here],
            send_sem=forward_send_sem.at[tiling, half],
            recv_sem=forward_recv_sem.at[tiling, half],
            device_id=device_across(tiling, (3 - axis,), to_core),
            device_id_type=MESH,
        )

    for n in range(CLASSES):
        first = 1 if n == 0 else 0
        group = recv.at[pl.ds(n * PER + first, PER - first)]
        pltpu.make_async_copy(group, group, recv_sem.at[n]).wait()
        arrived = recv[pl.ds(n * PER, PER)].reshape(CLASS_ROWS, width)
        for tiling in range(2):
            here = pl.ds(tiling * HALF, HALF)
            found = dot(place_of[n, here, :], arrived)
            if n == 0:
                gathered[here, :] = found
            elif n < CLASSES - 1:
                gathered[here, :] += found
            else:
                blocks[tiling, core] = (gathered[here, :] + found).astype(BF16)
                for axis in range(3):
                    neighbour_copy(tiling, axis, first_half(axis)).start()
                peer_copy(tiling).start()
                for axis in range(3):
                    neighbour_copy(tiling, axis, 1 - first_half(axis)).start()

    def score(tiling, key, query, same=False):
        key_slot, key_start, keys = key[:3]
        query_slot, query_start, queries = query[:3]
        products = dot(
            blocks[tiling, key_slot, pl.ds(key_start, keys), :],
            blocks[tiling, query_slot, pl.ds(query_start, queries), :],
            NT,
        )
        columns = slice(query_start, query_start + queries)
        key_no = iota((keys, queries), 0) + key_start
        allowed = key_no >= lows[tiling, query_slot][:, columns] - key[3] * HALF
        if same:
            allowed = allowed & (key_no < iota((keys, queries), 1) + query_start)
        found = jnp.max(jnp.where(allowed, products, -1.0), axis=0, keepdims=True)
        tops[tiling, query_slot, :, columns] = jnp.maximum(
            tops[tiling, query_slot, :, columns], found
        )

    def pair(tiling, a, b):
        a, b = (*a, number(tiling, a[0])), (*b, number(tiling, b[0]))
        a_first = a[3] < b[3]

        @pl.when(a_first)
        def _():
            score(tiling, a, b)

        @pl.when(jnp.logical_not(a_first))
        def _():
            score(tiling, b, a)

    def own_slot(tiling, axis):
        v1, v2, v3 = bits(tiling)
        return core ^ (0, v2, v2 ^ v3)[axis]

    def own_scores(tiling, carry):
        mine = (core, 0, HALF, number(tiling, core))
        score(tiling, mine, mine, True)
        peer = blocks.at[tiling, core ^ 1]
        pltpu.make_async_copy(peer, peer, peer_recv_sem.at[tiling]).wait()
        start = pl.multiple_of(core * QUARTER, QUARTER)
        key = (0, start, QUARTER, number(tiling, 0))
        score(tiling, key, (1, 0, HALF, number(tiling, 1)))
        return carry

    lax.fori_loop(0, 2, own_scores, 0)

    def wait_neighbour(tiling, axis, half):
        here = blocks.at[tiling, 2 + axis, pl.ds(half * QUARTER, QUARTER)]
        pltpu.make_async_copy(here, here, block_recv_sem.at[tiling, axis, half]).wait()

    def forward(tiling, carry):
        for axis in (1, 2):
            wait_neighbour(tiling, axis, first_half(axis))
            forward_copy(tiling, axis).start()
        return carry

    lax.fori_loop(0, 2, forward, 0)

    def held_part(axis, half):
        return (2 + axis, half * QUARTER, QUARTER)

    def first_scores(tiling, carry):
        wait_neighbour(tiling, 0, first_half(0))
        for axis in range(3):
            own = (own_slot(tiling, axis), 0, HALF)
            pair(tiling, own, held_part(axis, first_half(axis)))
        for axis, other in ((0, 1), (0, 2), (1, 2)):
            pair(
                tiling, held_part(axis, first_half(axis)), held_part(other, first_half(other))
            )
        return carry

    lax.fori_loop(0, 2, first_scores, 0)

    def second_scores(tiling, carry):
        for axis in range(3):
            wait_neighbour(tiling, axis, 1 - first_half(axis))
            own = (own_slot(tiling, axis), 0, HALF)
            pair(tiling, own, held_part(axis, 1 - first_half(axis)))
        for axis, other in ((0, 1), (0, 2), (1, 2)):
            pair(tiling, held_part(axis, 1 - first_half(axis)), (2 + other, 0, HALF))
            pair(
                tiling,
                held_part(axis, first_half(axis)),
                held_part(other, 1 - first_half(other)),
            )
        return carry

    lax.fori_loop(0, 2, second_scores, 0)

    zero_tiling = x & 1
    one_tiling = 1 - zero_tiling

    def stage(line, slot, tiling):
        for n in range(HALF // LANES):
            shares[line, n : n + 1, :] = tops[tiling, slot, :, n * LANES : (n + 1) * LANES]

    def send_found(line, target, owner, to_all, send_sem, recv_sem):
        source = shares.at[line]
        if line < 9:
            place = early.at[owner * 9 + line]
        else:
            place = late.at[owner * 2 + line - 9]

        def send_one(m, carry):
            pltpu.make_async_remote_copy(
                src_ref=source,
                dst_ref=place,
                send_sem=send_sem,
                recv_sem=recv_sem,
                device_id=(target, grp_at(m, 1)),
                device_id_type=MESH,
            ).start()
            return carry

        lax.fori_loop(0 if to_all else 1, GRP, send_one, 0)
        if not to_all:
            place[...] = source[...]

    for tiling in range(2):
        v2 = bits(tiling)[1]
        for kind, slot in enumerate((core, core ^ 1, 3, 4)):
            stage(tiling * 4 + kind, slot, tiling)
        line = tiling * 4
        send_found(line, src, grp, False, early_send_sem, early_recv_sem)
        send_found(line + 1, src, grp ^ 1, False, early_send_sem, early_recv_sem)
        target, owner = device_across(tiling, (1,), core)
        send_found(line + 2, target, owner, True, early_send_sem, early_recv_sem)
        target, owner = device_across(tiling, (2,), core ^ v2)
        send_found(line + 3, src, owner, False, early_send_sem, early_recv_sem)
    stage(8, 2, one_tiling)
    target, owner = device_across(one_tiling, (0,), core ^ 1)
    send_found(8, target, owner, True, early_send_sem, early_recv_sem)

    def far_scores(tiling, carry):
        for half in range(2):
            here = blocks.at[tiling, 5, pl.ds(half * QUARTER, QUARTER)]
            pltpu.make_async_copy(here, here, forward_recv_sem.at[tiling, half]).wait()
            pair(tiling, (2, 0, HALF), (5, half * QUARTER, QUARTER))
        return carry

    far_scores(zero_tiling, 0)
    stage(9, 2, zero_tiling)
    target, owner = device_across(zero_tiling, (0,), core)
    send_found(9, target, owner, True, late_send_sem, late_recv_sem)
    far_scores(one_tiling, 0)
    stage(10, 5, one_tiling)
    target, owner = device_across(one_tiling, (1, 2), core)
    send_found(10, target, owner, True, late_send_sem, late_recv_sem)

    def wait_early(sem):
        here = early.at[pl.ds(0, EARLY)]
        pltpu.make_async_copy(here, here, sem).wait()

    wait_early(early_recv_sem)
    for owner in range(GRP):
        for tiling in range(2):
            line = owner * 9 + tiling * 4
            early[line] = jnp.maximum(
                jnp.maximum(early[line], early[line + 1]),
                jnp.maximum(early[line + 2], early[line + 3]),
            )
    pltpu.make_async_copy(late, late, late_recv_sem).wait()
    for owner in range(GRP):
        line = owner * 9
        to_zero, to_one = early[line + 8], jnp.maximum(late[owner * 2], late[owner * 2 + 1])
        added = (
            jnp.maximum(early[line], jnp.where(zero_tiling == 0, to_zero, to_one)),
            jnp.maximum(early[line + 4], jnp.where(zero_tiling == 0, to_one, to_zero)),
        )
        best[owner] = jnp.concatenate(added, axis=0)

    lines = GRP * rows // LANES
    parts = jnp.concatenate(three_parts(best[...].reshape(lines, LANES)), axis=0)
    answer = dot(parts, look[...])
    answer = answer[:lines] + answer[lines : 2 * lines] + answer[2 * lines :]
    right = iota(answer.shape, 0) == pick_row
    answer = jnp.sum(jnp.where(right, answer, 0.0), axis=0, keepdims=True)
    for n in range(SRC):
        answers[n] = answer[:, n * LANES : (n + 1) * LANES]
    returned[0] = answers[0]

    def send_answer(n, carry):
        pltpu.make_async_remote_copy(
            src_ref=answers.at[n],
            dst_ref=returned.at[n],
            send_sem=answer_send_sem,
            recv_sem=answer_recv_sem,
            device_id=(src_at(n, -1), grp),
            device_id_type=MESH,
        ).start()
        return carry

    lax.fori_loop(1, SRC, send_answer, 0)
    wait_all(returned, answer_recv_sem, SRC - 1)
    table = returned[...].reshape(SRC, LANES).T
    parts = jnp.concatenate(three_parts(table), axis=1)
    chosen = dot(parts, jnp.concatenate([to_column] * 3, axis=0))
    out[...] = jnp.sum(chosen * lane_hot.astype(F32), axis=0, keepdims=True)

    wait_all(sent_meta, column_send_sem, SRC - 1)
    wait_all(group_meta, group_send_sem, GRP - 1)
    wait_early(early_send_sem)
    pltpu.make_async_copy(late, late, late_send_sem).wait()
    wait_all(answers, answer_send_sem, SRC - 1)
    for n in range(CLASSES):
        first = 1 if n == 0 else 0
        group = send.at[pl.ds(n * PER + first, PER - first)]
        pltpu.make_async_copy(group, group, send_sem.at[n]).wait()
    for tiling in range(2):
        whole = blocks.at[tiling, core]
        pltpu.make_async_copy(whole, whole, peer_send_sem.at[tiling]).wait()
        for half in range(2):
            here = blocks.at[tiling, core, pl.ds(half * QUARTER, QUARTER)]
            for axis in range(3):
                pltpu.make_async_copy(here, here, block_send_sem.at[tiling, axis, half]).wait()
            pltpu.make_async_copy(here, here, forward_send_sem.at[tiling, half]).wait()


def on_device(embeds, cluster_id, cluster_rank, cluster_size):
    rows, width = embeds.shape
    clusters = cluster_size.shape[0]
    best = pl.pallas_call(
        kernel,
        out_shape=jax.ShapeDtypeStruct((1, rows), F32),
        in_specs=[pl.BlockSpec(memory_space=pl.ANY)] * 4,
        out_specs=pl.BlockSpec(memory_space=pltpu.VMEM),
        scratch_shapes=[
            pltpu.VMEM((rows, width), BF16),
            pltpu.VMEM((1, rows), jnp.int32),
            pltpu.VMEM((1, rows), jnp.int32),
            pltpu.VMEM((1, clusters), jnp.int32),
            pltpu.VMEM((rows, width), BF16),
            pltpu.VMEM((DEVICES, SLOTS, width), BF16),
            pltpu.VMEM((DEVICES, SLOTS, width), BF16),
            pltpu.VMEM((SRC, 1, LANES), F32),
            pltpu.VMEM((SRC, 1, LANES), F32),
            pltpu.VMEM((GRP, SRC, 1, LANES), F32),
            pltpu.VMEM((CLASSES, rows, CLASS_ROWS), BF16),
            pltpu.VMEM((LANES, SRC * LANES), BF16),
            pltpu.VMEM((rows, width), F32),
            pltpu.VMEM((2, HELD, HALF, width), BF16),
            pltpu.VMEM((2, HELD, 1, HALF), F32),
            pltpu.VMEM((2, HELD, 1, HALF), jnp.int32),
            pltpu.VMEM((11, HALF // LANES, LANES), F32),
            pltpu.VMEM((GRP * 9, HALF // LANES, LANES), F32),
            pltpu.VMEM((GRP * 2, HALF // LANES, LANES), F32),
            pltpu.VMEM((GRP, rows // LANES, LANES), F32),
            pltpu.VMEM((SRC, 1, LANES), F32),
            pltpu.VMEM((SRC, 1, LANES), F32),
            pltpu.SemaphoreType.DMA((4,)),
            pltpu.SemaphoreType.REGULAR,
            pltpu.SemaphoreType.DMA((CLASSES,)),
            pltpu.SemaphoreType.DMA((CLASSES,)),
            pltpu.SemaphoreType.DMA,
            pltpu.SemaphoreType.DMA,
            pltpu.SemaphoreType.DMA,
            pltpu.SemaphoreType.DMA,
            pltpu.SemaphoreType.DMA((2, 3, 2)),
            pltpu.SemaphoreType.DMA((2, 3, 2)),
            pltpu.SemaphoreType.DMA((2,)),
            pltpu.SemaphoreType.DMA((2,)),
            pltpu.SemaphoreType.DMA((2, 2)),
            pltpu.SemaphoreType.DMA((2, 2)),
            pltpu.SemaphoreType.DMA,
            pltpu.SemaphoreType.DMA,
            pltpu.SemaphoreType.DMA,
            pltpu.SemaphoreType.DMA,
            pltpu.SemaphoreType.DMA,
            pltpu.SemaphoreType.DMA,
        ],
        compiler_params=pltpu.CompilerParams(
            collective_id=0, has_side_effects=True, vmem_limit_bytes=50 * 1024 * 1024
        ),
        name="dedup",
    )(
        embeds,
        cluster_id.reshape(1, rows),
        cluster_rank.reshape(1, rows),
        cluster_size.reshape(1, -1),
    )
    return best.reshape(rows)


def solution(mesh):
    placed = (P(("src", "grp"), None), P(("src", "grp")), P(("src", "grp")), P())
    return jax.shard_map(
        on_device, mesh=mesh, in_specs=placed, out_specs=P(("src", "grp")), check_vma=False
    )
```
